128 devices in a mesh: dp: 4 (over y), seq: 32 (over z, x, core).
Axes of the slice: x: 4, y: 4, z: 4, core: 2. Of those that a mesh axis runs over, the one named last changes fastest.
Arguments:
- query: bfloat16 [16384, 3072], P(('dp', 'seq')), parts along dimension 0, may hold values from -24 to 24
- key_in: bfloat16 [16384, 3072], P(('dp', 'seq')), parts along dimension 0, may hold values from -24 to 24
- value: bfloat16 [16384, 3072], P(('dp', 'seq')), parts along dimension 0, may hold values from -6 to 6
- grad_out: bfloat16 [16384, 3072], P(('dp', 'seq')), parts along dimension 0, may hold values from -6 to 6
- masks: int32 [96, 32, 32], P('dp'), parts along dimension 0, may hold values from 0 to 1, as said below
Outputs:
- attn_out: bfloat16 [16384, 3072], P(('dp', 'seq')), parts along dimension 0
- grad_query: bfloat16 [16384, 3072], P(('dp', 'seq')), parts along dimension 0
- grad_key: bfloat16 [16384, 3072], P(('dp', 'seq')), parts along dimension 0
- grad_value: bfloat16 [16384, 3072], P(('dp', 'seq')), parts along dimension 0
The draws below stay inside these ranges and needn't reach their ends.
There are 4 independent parts, one for each index of `dp`. The reference program is written for one: setup_inputs(seed, part) draws one part's arguments, and reference() takes and returns one part's arrays. A program takes and returns all parts, laid end to end along the dimension named above; each array names one. Nothing has to cross between parts.
Inputs may be any that keep to these rules, and one draw needn't show every extreme that they name: masks[h, i, i] is 1 for every head h and block i.
All inputs are finite; a program needn't handle non-finite values.
Results may differ from the reference program's by a relative error of at most 0.012.
Values may be sent and summed in bfloat16 or wider, within the bound.
No kernel may reach another device: no remote copies, remote signals or barrier semaphores. Data moves between devices by JAX's collectives and lax.ppermute only.
A program may use at most 128 MiB of HBM per device.

```python
import jax
import jax.numpy as jnp
from jax import lax

HEADS = 24
HEAD_DIM = 128
TILE = 128
SEQ = 4096
BLOCKS = 32
ITEMS = 48


def draw_query(key, part):
    key = jax.random.fold_in(key, 1)
    values = jnp.clip(jax.random.normal(key, (SEQ, HEADS * HEAD_DIM), jnp.float32), -4.0, 4.0)
    return values.astype(jnp.bfloat16)


def draw_key_in(key, part):
    key = jax.random.fold_in(key, 2)
    values = jnp.clip(jax.random.normal(key, (SEQ, HEADS * HEAD_DIM), jnp.float32), -4.0, 4.0)
    return values.astype(jnp.bfloat16)


def draw_masks(key, part):
    key = jax.random.fold_in(key, 5)
    level_key, cell_key = jax.random.split(key)
    levels = jax.random.randint(level_key, (HEADS, 1, 1), 1, 11)
    cells = jax.random.randint(cell_key, (HEADS, BLOCKS, BLOCKS), 0, 10)
    diagonal = jnp.eye(BLOCKS, dtype=jnp.int32)[None]
    return jnp.maximum((cells < levels).astype(jnp.int32), diagonal)


def block_levels(key, shape, shards, least, largest):
    def one(dim, blocks):
        steps = jax.random.uniform(jax.random.fold_in(jax.random.fold_in(key, 6), dim), (blocks,), jnp.float32, least / len(shards), largest / len(shards))
        return jnp.repeat(jnp.exp(steps), shape[dim] // blocks).reshape((-1,) + (1,) * (len(shape) - dim - 1))

    level = one(*shards[0])
    for cut in shards[1:]:
        level = level * one(*cut)
    return level


def scatter_about(rng, dims, scale, bound, shards=(), held_as=jnp.bfloat16):
    result = scale * jax.random.normal(rng, dims, jnp.float32)
    if shards:
        result = result * block_levels(rng, dims, shards, -0.22, 0.18)
    return jnp.clip(result, -bound, bound).astype(held_as)


def setup_inputs(seed: int = 0, part: int = 0) -> dict:
    arg_keys = jax.random.split(jax.random.key(seed), 6)
    part_keys = jax.random.split(jax.random.fold_in(arg_keys[5], part), 6)
    return {
        "query": draw_query(jax.random.fold_in(jax.random.fold_in(arg_keys[5], part), 71), part),
        "key_in": draw_key_in(jax.random.fold_in(jax.random.fold_in(arg_keys[5], part), 71), part),
        "value": scatter_about(part_keys[2], (SEQ, HEADS * HEAD_DIM), 1.0, 6.0, ((0, 32),)),
        "grad_out": scatter_about(part_keys[3], (SEQ, HEADS * HEAD_DIM), 1.0, 6.0, ((0, 32),)),
        "masks": draw_masks(jax.random.fold_in(jax.random.fold_in(arg_keys[5], part), 71), part),
    }


def attend(q_rows, keys, values, grads, mask_rows):
    rows_total, width = q_rows.shape
    scale = width ** -0.5
    q_wide = q_rows.astype(jnp.float32)
    k_wide = keys.astype(jnp.float32)
    v_wide = values.astype(jnp.float32)
    g_wide = grads.astype(jnp.float32)
    scores = jnp.dot(q_wide, k_wide.T, preferred_element_type=jnp.float32) * scale
    live = (mask_rows > 0)[:, None, :, None]
    shaped = scores.reshape(rows_total // TILE, TILE, BLOCKS, TILE)
    scores = jnp.where(live, shaped, -jnp.inf).reshape(rows_total, SEQ)
    highest = jnp.max(scores, axis=1, keepdims=True)
    raised = jnp.exp(scores - highest)
    probs = raised / jnp.sum(raised, axis=1, keepdims=True)
    probs_low = lax.optimization_barrier(probs.astype(jnp.bfloat16)).astype(jnp.float32)
    out_rows = jnp.dot(probs_low, v_wide, preferred_element_type=jnp.float32)
    delta = jnp.sum(g_wide * out_rows, axis=1, keepdims=True)
    grad_probs = jnp.dot(g_wide, v_wide.T, preferred_element_type=jnp.float32)
    grad_scores = lax.optimization_barrier((probs * (grad_probs - delta)).astype(jnp.bfloat16)).astype(jnp.float32)
    query_grad = (scale * jnp.dot(grad_scores, k_wide, preferred_element_type=jnp.float32)).astype(jnp.bfloat16)
    key_part = (scale * jnp.dot(grad_scores.T, q_wide, preferred_element_type=jnp.float32)).astype(jnp.bfloat16)
    value_part = jnp.dot(probs_low.T, g_wide, preferred_element_type=jnp.float32).astype(jnp.bfloat16)
    return out_rows.astype(jnp.bfloat16), query_grad, key_part, value_part


def reference(query, key_in, value, grad_out, masks):
    half_rows = SEQ // 2
    q_heads = query.reshape(SEQ, HEADS, HEAD_DIM)
    k_heads = key_in.reshape(SEQ, HEADS, HEAD_DIM)
    v_heads = value.reshape(SEQ, HEADS, HEAD_DIM)
    g_heads = grad_out.reshape(SEQ, HEADS, HEAD_DIM)

    def one_item(item):
        head = item // 2
        half = item % 2
        start = (half * half_rows).astype(jnp.int32)
        q_head = lax.dynamic_index_in_dim(q_heads, head, 1, keepdims=False)
        k_head = lax.dynamic_index_in_dim(k_heads, head, 1, keepdims=False)
        v_head = lax.dynamic_index_in_dim(v_heads, head, 1, keepdims=False)
        g_head = lax.dynamic_index_in_dim(g_heads, head, 1, keepdims=False)
        q_rows = lax.dynamic_slice_in_dim(q_head, start, half_rows, 0)
        g_rows = lax.dynamic_slice_in_dim(g_head, start, half_rows, 0)
        mask_head = lax.dynamic_index_in_dim(masks, head, 0, keepdims=False)
        mask_start = (half * (half_rows // TILE)).astype(jnp.int32)
        mask_rows = lax.dynamic_slice_in_dim(mask_head, mask_start, half_rows // TILE, 0)
        return attend(q_rows, k_head, v_head, g_rows, mask_rows)

    outs, query_grads, key_parts, value_parts = lax.map(one_item, jnp.arange(ITEMS, dtype=jnp.int32))

    def rows_layout(stacked):
        return stacked.reshape(HEADS, SEQ, HEAD_DIM).transpose(1, 0, 2).reshape(SEQ, HEADS * HEAD_DIM)

    def pair_sum(parts):
        total = parts.reshape(HEADS, 2, SEQ, HEAD_DIM).astype(jnp.float32).sum(axis=1)
        return total.astype(jnp.bfloat16).transpose(1, 0, 2).reshape(SEQ, HEADS * HEAD_DIM)

    return rows_layout(outs), rows_layout(query_grads), pair_sum(key_parts), pair_sum(value_parts)
```

```python
import functools

import jax
import jax.numpy as jnp
from jax import lax
from jax.experimental import pallas as pl
from jax.experimental.pallas import tpu as pltpu
from jax.sharding import PartitionSpec as P

NT = (((1,), (1,)), ((), ()))
NN = (((1,), (0,)), ((), ()))
LOG2E = 1.4426950408889634


def dense_kernel(ck, split, bias_ref, own_ref, oth_ref, rows_ref, keep_ref, give_ref,
                 k_scr, v_scr, kt_scr, vt_scr, dk_scr, dv_scr, p0_scr, p1_scr, m_scr, qg_scr):
    half, slots, tile, width = own_ref.shape
    keys = 2 * half * tile
    lanes = 2 * tile
    tiles = bias_ref.shape[0]
    chunks = keys // ck
    sub = ck // tile
    scale = width ** -0.5
    c2 = scale * LOG2E
    ks = slots - 2
    f32, bf16 = jnp.float32, jnp.bfloat16
    per = 4 if split else 2
    hr = lanes // per

    def dot(a, b, dims=NN):
        return lax.dot_general(a, b, dims, preferred_element_type=f32)

    def prep(c, _):
        for src, base, s0 in ((own_ref, 0, ks), (oth_ref, half, 0)):
            k = src[c, s0]
            v = src[c, s0 + 1]
            at = pl.ds(pl.multiple_of((base + c) * tile, tile), tile)
            k_scr[at, :] = k
            v_scr[at, :] = v
            kt_scr[:, at] = k.T
            vt_scr[:, at] = v.T
            dk_scr[at, :] = jnp.zeros((tile, width), f32)
            dv_scr[at, :] = jnp.zeros((tile, width), f32)
        return 0

    lax.fori_loop(0, half, prep, 0)

    def q_tile(t):
        if split:
            return jnp.concatenate([own_ref[per * t + i, 0, :hr] for i in range(per)], 0)
        return jnp.concatenate([own_ref[per * t + i, 0] for i in range(per)], 0)

    def g_tile(t):
        if split:
            return jnp.concatenate([own_ref[per * t + i, 0, hr:] for i in range(per)], 0)
        return jnp.concatenate([own_ref[per * t + i, 1] for i in range(per)], 0)

    def put(t, slot, x):
        for i in range(per):
            part = x[i * hr:(i + 1) * hr].astype(bf16)
            if split:
                rows_ref[per * t + i, 0, slot * hr:(slot + 1) * hr] = part
            else:
                rows_ref[per * t + i, slot] = part

    def forward(t, c, p_ref, m_at, carry):
        m, l, o = carry
        at = pl.ds(pl.multiple_of(c * ck, ck), ck)
        s = dot(k_scr[at, :], q_tile(t), NT)
        bias = bias_ref[t, pl.ds(pl.multiple_of(c * sub, sub), sub), :]
        x = s.reshape(sub, tile, lanes) * c2 + bias[:, None, :]
        top = jnp.max(x.reshape(ck // 8, 8, lanes), axis=0)
        new = jnp.maximum(m, jnp.max(top, axis=0, keepdims=True))
        alpha = jnp.exp2(m - new)
        p = jnp.exp2(x.reshape(ck, lanes) - new)
        l = l * alpha + jnp.sum(jnp.sum(p.reshape(ck // 8, 8, lanes), axis=0), axis=0, keepdims=True)
        pb = p.astype(bf16)
        p_ref[at, :] = pb
        m_scr[m_at, pl.ds(c, 1), :] = new
        o = o * alpha + dot(vt_scr[:, at], pb)
        return new, l, o

    def start():
        return jnp.full((1, lanes), -1e30, f32), jnp.zeros((1, lanes), f32), jnp.zeros((width, lanes), f32)

    def close(t, m_at, carry):
        m, l, o = carry
        rl = 1.0 / l
        ot = o * rl
        put(t, 0, ot.T)
        delta = jnp.sum(g_tile(t).astype(f32).T * ot, axis=0, keepdims=True)
        m_scr[m_at, 0:chunks, :] = jnp.exp2(m_scr[m_at, 0:chunks, :] - m) * rl
        return delta

    def backward(t, c, p_ref, m_at, delta, dq):
        at = pl.ds(pl.multiple_of(c * ck, ck), ck)
        g = g_tile(t)
        q = q_tile(t)
        p = p_ref[at, :].astype(f32) * m_scr[m_at, pl.ds(c, 1), :]
        dp = dot(v_scr[at, :], g, NT)
        ds = (p * (dp - delta)).astype(bf16)
        dv_scr[at, :] += dot(p.astype(bf16), g)
        dk_scr[at, :] += dot(ds, q)
        return dq + dot(kt_scr[:, at], ds)

    zero_q = jnp.zeros((width, lanes), f32)
    refs = (p0_scr, p1_scr)

    first = lax.fori_loop(0, chunks, lambda c, x: forward(0, c, refs[0], 0, x), start())
    delta = close(0, 0, first)

    def both(t, cur, delta):
        def step(c, x):
            fwd, dq = x
            dq = backward(t - 1, c, refs[1 - cur], 1 - cur, delta, dq)
            fwd = forward(t, c, refs[cur], cur, fwd)
            return fwd, dq
        fwd, dq = lax.fori_loop(0, chunks, step, (start(), zero_q))
        put(t - 1, 1, (dq * scale).T)
        return close(t, cur, fwd)

    def pair(i, delta):
        delta = both(2 * i + 1, 1, delta)
        return both(2 * i + 2, 0, delta)

    delta = lax.fori_loop(0, tiles // 2 - 1, pair, delta)
    delta = both(tiles - 1, 1, delta)
    dq = lax.fori_loop(0, chunks, lambda c, x: backward(tiles - 1, c, refs[1], 1, delta, x), zero_q)
    put(tiles - 1, 1, (dq * scale).T)

    def finish(c, _):
        for base, ref in ((0, keep_ref), (half, give_ref)):
            at = pl.ds(pl.multiple_of((base + c) * tile, tile), tile)
            ref[c, 0] = (dk_scr[at, :] * scale).astype(bf16)
            ref[c, 1] = dv_scr[at, :].astype(bf16)
        return 0

    lax.fori_loop(0, half, finish, 0)


CHUNK = 2048


def attend_call(bias, own, oth, split, chunk=CHUNK):
    half, slots, tile, width = own.shape
    keys = 2 * half * tile
    rows = bias.shape[0] * bias.shape[2]
    f32, bf16 = jnp.float32, jnp.bfloat16
    vm = pl.BlockSpec(memory_space=pltpu.VMEM)
    return pl.pallas_call(
        functools.partial(dense_kernel, chunk, split),
        out_shape=(
            jax.ShapeDtypeStruct((half, slots - 2, tile, width), bf16),
            jax.ShapeDtypeStruct((half, 2, tile, width), bf16),
            jax.ShapeDtypeStruct((half, 2, tile, width), bf16),
        ),
        in_specs=[vm, vm, vm],
        out_specs=[vm, vm, vm],
        scratch_shapes=[
            pltpu.VMEM((keys, width), bf16),
            pltpu.VMEM((keys, width), bf16),
            pltpu.VMEM((width, keys), bf16),
            pltpu.VMEM((width, keys), bf16),
            pltpu.VMEM((keys, width), f32),
            pltpu.VMEM((keys, width), f32),
            pltpu.VMEM((keys, 2 * tile), bf16),
            pltpu.VMEM((keys, 2 * tile), bf16),
            pltpu.VMEM((2, 32, 2 * tile), f32),
            pltpu.VMEM((8, 128), f32),
        ],
        compiler_params=pltpu.CompilerParams(vmem_limit_bytes=40 * 2**20),
        cost_estimate=pl.CostEstimate(
            flops=12 * rows * keys * width, bytes_accessed=8 * keys * width * 2, transcendentals=rows * keys
        ),
    )(bias, own, oth)


def pack_kernel(chips, split, width, q_ref, k_ref, v_ref, g_ref, out_ref):
    rows = q_ref.shape[0]
    for i in range(chips):
        if split:
            part = i % 2
            at = slice(i // 2 * width, (i // 2 + 1) * width)
            cut = slice(part * (rows // 2), (part + 1) * (rows // 2))
            out_ref[i, 0, : rows // 2] = q_ref[cut, at]
            out_ref[i, 0, rows // 2 :] = g_ref[cut, at]
            out_ref[i, 1] = k_ref[:, at]
            out_ref[i, 2] = v_ref[:, at]
        else:
            at = slice(i * width, (i + 1) * width)
            out_ref[i, 0] = q_ref[:, at]
            out_ref[i, 1] = g_ref[:, at]
            out_ref[i, 2] = k_ref[:, at]
            out_ref[i, 3] = v_ref[:, at]


def pack_call(arrays, chips, split, width):
    rows, columns = arrays[0].shape
    whole = chips * width
    rest = columns - whole
    slots = 3 if split else 4
    if split:
        spec = pl.BlockSpec((rows, rest), lambda i: (0, whole // rest))
    else:
        spec = pl.BlockSpec((rows, whole), lambda i: (0, 0))
    return pl.pallas_call(
        functools.partial(pack_kernel, chips, split, width),
        grid=(1,),
        out_shape=jax.ShapeDtypeStruct((chips, slots, rows, width), jnp.bfloat16),
        in_specs=[spec] * 4,
        out_specs=pl.BlockSpec((chips, slots, rows, width), lambda i: (0, 0, 0, 0)),
        compiler_params=pltpu.CompilerParams(vmem_limit_bytes=24 * 2**20),
    )(*arrays)


def unpack_kernel(chips, width, a_ref, b_ref, out_ref, query_ref, key_ref, value_ref):
    rows = out_ref.shape[0]
    outs = (out_ref, query_ref, key_ref, value_ref)
    for i in range(chips):
        at = slice(i * width, (i + 1) * width)
        for s in range(4):
            outs[s][:, at] = a_ref[i, s]
    for i in range(chips // 2):
        at = slice((chips + i) * width, (chips + i + 1) * width)
        for s in range(2):
            cut = slice(s * (rows // 2), (s + 1) * (rows // 2))
            for part in range(2):
                outs[s][part * (rows // 2) : (part + 1) * (rows // 2), at] = b_ref[2 * i + part, 0, cut]
            one = b_ref[2 * i, 1 + s].astype(jnp.float32) + b_ref[2 * i + 1, 1 + s].astype(jnp.float32)
            outs[2 + s][:, at] = one.astype(jnp.bfloat16)


def unpack_call(back_a, back_b, heads):
    chips, _, rows, width = back_a.shape
    vm = pl.BlockSpec(memory_space=pltpu.VMEM)
    return pl.pallas_call(
        functools.partial(unpack_kernel, chips, width),
        out_shape=[jax.ShapeDtypeStruct((rows, heads * width), jnp.bfloat16)] * 4,
        in_specs=[vm, vm],
        out_specs=[vm] * 4,
        compiler_params=pltpu.CompilerParams(vmem_limit_bytes=24 * 2**20),
    )(back_a, back_b)


def body(query, key_in, value, grad_out, masks):
    peers = lax.axis_size("seq")
    chips = peers // 2
    position = lax.axis_index("seq")
    chip, core = position // 2, position % 2
    heads, blocks = masks.shape[:2]
    width = query.shape[1] // heads
    tile = query.shape[0]
    groups = [list(range(e, peers, 2)) for e in range(2)]
    swap = [(i, i ^ 1) for i in range(peers)]

    def exchange(array):
        return lax.all_to_all(array, "seq", 0, 0, axis_index_groups=groups, tiled=True)

    def bias_of(head, per):
        live = lax.dynamic_index_in_dim(masks, head, 0, keepdims=False).reshape(chips, 2, chips, 2)
        live = lax.dynamic_index_in_dim(live, core, 1, keepdims=False)
        live = jnp.where(core == 0, live, live[:, :, ::-1])
        live = live.transpose(0, 2, 1).reshape(chips // per, per, blocks).transpose(0, 2, 1)
        bias = jnp.where(live > 0, 0.0, -1e30).astype(jnp.float32)
        return jnp.repeat(bias, 2 * tile // per, axis=2)

    arrays = (query, key_in, value, grad_out)
    got_b = exchange(pack_call(arrays, chips, True, width))
    got_a = exchange(pack_call(arrays, chips, False, width))
    bias_b = bias_of(chips + chip // 2, 4)
    bias_a = bias_of(chip, 2)

    def run(got, bias, split):
        other = lax.ppermute(got[:, got.shape[1] - 2 :], "seq", swap)
        rows, keep, give = attend_call(bias, got, other, split)
        taken = lax.ppermute(give, "seq", swap)
        total = (keep.astype(jnp.float32) + taken.astype(jnp.float32)).astype(jnp.bfloat16)
        return exchange(jnp.concatenate([rows, total], axis=1))

    back_b = run(got_b, bias_b, True)
    back_a = run(got_a, bias_a, False)
    return tuple(unpack_call(back_a, back_b, heads))


def solution(mesh):
    tokens = P(("dp", "seq"), None)
    return jax.shard_map(
        body,
        mesh=mesh,
        in_specs=(tokens, tokens, tokens, tokens, P("dp", None, None)),
        out_specs=(tokens, tokens, tokens, tokens),
        check_vma=False,
    )
```

```python
import functools

import jax
import jax.numpy as jnp
from jax import lax
from jax.experimental import pallas as pl
from jax.experimental.pallas import tpu as pltpu
from jax.sharding import PartitionSpec as P

LANES = 512
BLOCK = 256
STEP = 4096
NT = (((1,), (1,)), ((), ()))
NN = (((1,), (0,)), ((), ()))
LOG2E = 1.4426950408889634


def at_multiple(x, n):
    return x if isinstance(x, int) else pl.multiple_of(x, n)


def dense_kernel(block, step_rows, lanes, split, live_ref, own_ref, oth_ref, rows_ref, give_ref,
                 k_scr, v_scr, kt_scr, vt_scr, dk_scr, dv_scr, x_scr, p_scr, bias_ref):
    half, slots, tile, width = own_ref.shape
    keys = 2 * half * tile
    queries = half * tile // (2 if split else 1)
    tiles = queries // lanes
    scale = width ** -0.5
    c2 = scale * LOG2E
    ks = slots - 2
    f32, bf16 = jnp.float32, jnp.bfloat16
    per = lanes // tile * (2 if split else 1)
    hr = lanes // per
    subs = step_rows // block
    tall = vt_scr.shape[0]

    def dot(a, b, dims=NN):
        return lax.dot_general(a, b, dims, preferred_element_type=f32)

    def prep(c, _):
        for src, base, s0 in ((own_ref, 0, ks), (oth_ref, half, oth_ref.shape[1] - 2)):
            k = src[c, s0]
            v = src[c, s0 + 1]
            at = pl.ds(pl.multiple_of((base + c) * tile, tile), tile)
            k_scr[at, :] = k
            v_scr[at, :] = v
            kt_scr[:, at] = k.T
            vt_scr[0:width, at] = v.T
            vt_scr[width:, at] = jnp.ones((tall - width, tile), bf16)
            dk_scr[at, :] = jnp.zeros((tile, width), f32)
            dv_scr[at, :] = jnp.zeros((tile, width), f32)
        return 0

    lax.fori_loop(0, half, prep, 0)
    lane = lax.broadcasted_iota(jnp.int32, (half, lanes), 1)
    row = lax.broadcasted_iota(jnp.int32, (half, lanes), 0)
    for t in range(tiles):
        spread = (lane // hr + per * t == row).astype(f32).astype(bf16)
        bias_ref[t] = jnp.where(dot(live_ref[...], spread) > 0.5, 0.0, -1e30)

    def q_tile(t):
        if split:
            return jnp.concatenate([own_ref[per * t + i, 0, :hr] for i in range(per)], 0)
        return jnp.concatenate([own_ref[per * t + i, 0] for i in range(per)], 0)

    def g_tile(t):
        if split:
            return jnp.concatenate([own_ref[per * t + i, 0, hr:] for i in range(per)], 0)
        return jnp.concatenate([own_ref[per * t + i, 1] for i in range(per)], 0)

    def put(t, slot, x):
        for i in range(per):
            part = x[i * hr : (i + 1) * hr].astype(bf16)
            if split:
                rows_ref[per * t + i, 0, slot * hr : (slot + 1) * hr] = part
            else:
                rows_ref[per * t + i, slot] = part

    def stage(t):
        scores, probs, grads = t + 1 < tiles, 0 <= t < tiles, 0 <= t - 1
        q_next = q_tile(t + 1) if scores else None
        if grads:
            g, (qn, gn, delta, _) = g_tile(t - 1), closed[t - 1]
        if probs:
            top = jnp.max(tops[t], axis=0, keepdims=True) * c2

        def step(i, carry):
            best, o, dq = carry
            at = pl.ds(at_multiple(i * step_rows, step_rows), step_rows)
            ds_all, p_all = [], []
            for u in range(subs):
                row = at_multiple(i * step_rows + u * block, block)
                sub = pl.ds(row, block)
                if grads:
                    pb = p_scr[sub, :]
                    dp = dot(v_scr[sub, :], g, NT)
                    ds = pb * (dp - delta).astype(bf16)
                    dv_scr[sub, :] += dot(pb, gn)
                    dk_scr[sub, :] += dot(ds, qn)
                    ds_all.append(ds)
                if probs:
                    pb = jnp.exp2(x_scr[sub, :] * c2 - top).astype(bf16)
                    p_scr[sub, :] = pb
                    p_all.append(pb)
                if scores:
                    s = dot(k_scr[sub, :], q_next, NT).reshape(block // tile, tile, lanes)
                    for w in range(block // tile):
                        x = s[w] + bias_ref[t + 1, pl.ds(i * (step_rows // tile) + u * (block // tile) + w, 1), :]
                        x_scr[pl.ds(at_multiple(row + w * tile, tile), tile), :] = x
                        best = jnp.maximum(best, jnp.max(x.reshape(tile // 8, 8, lanes), axis=0))
            if grads:
                dq = dq + dot(kt_scr[:, at], jnp.concatenate(ds_all, 0))
            if probs:
                o = o + dot(vt_scr[:, at], jnp.concatenate(p_all, 0))
            return best, o, dq

        start = (
            jnp.full((8, lanes), -1e30, f32) if scores else 0,
            jnp.zeros((tall, lanes), f32) if probs else 0,
            jnp.zeros((width, lanes), f32) if grads else 0,
        )
        best, o, dq = step(0, start) if keys == step_rows else lax.fori_loop(0, keys // step_rows, step, start)
        if scores:
            tops[t + 1] = best
        if grads:
            put(t - 1, 1, (dq * (closed[t - 1][3] * scale)).T)
        if probs:
            rl = 1.0 / o[width : width + 1]
            ot = o[:width] * rl
            put(t, 0, ot.T)
            gf = g_tile(t).astype(f32)
            delta = jnp.sum(gf.T * ot, axis=0, keepdims=True)
            column = jnp.broadcast_to(rl, (width, lanes)).T
            closed[t] = ((q_tile(t).astype(f32) * column).astype(bf16), (gf * column).astype(bf16), delta, rl)

    tops, closed = {}, {}
    for t in range(-1, tiles + 1):
        stage(t)

    def finish(c, _):
        for base, ref, slot in ((0, rows_ref, slots - 2), (half, give_ref, 0)):
            at = pl.ds(pl.multiple_of((base + c) * tile, tile), tile)
            ref[c, slot] = (dk_scr[at, :] * scale).astype(bf16)
            ref[c, slot + 1] = dv_scr[at, :].astype(bf16)
        return 0

    lax.fori_loop(0, half, finish, 0)


def attend_call(live, own, oth, split):
    half, slots, tile, width = own.shape
    keys = 2 * half * tile
    rows = half * tile // (2 if split else 1)
    lanes = min(LANES, rows)
    f32, bf16 = jnp.float32, jnp.bfloat16
    vm = pl.BlockSpec(memory_space=pltpu.VMEM)
    return pl.pallas_call(
        functools.partial(dense_kernel, BLOCK, min(STEP, keys), lanes, split),
        out_shape=(
            jax.ShapeDtypeStruct((half, slots, tile, width), bf16),
            jax.ShapeDtypeStruct((half, 2, tile, width), bf16),
        ),
        in_specs=[vm, vm, vm],
        out_specs=[vm, vm],
        scratch_shapes=[
            pltpu.VMEM((keys, width), bf16),
            pltpu.VMEM((keys, width), bf16),
            pltpu.VMEM((width, keys), bf16),
            pltpu.VMEM((width + 16, keys), bf16),
            pltpu.VMEM((keys, width), f32),
            pltpu.VMEM((keys, width), f32),
            pltpu.VMEM((keys, lanes), f32),
            pltpu.VMEM((keys, lanes), bf16),
            pltpu.VMEM((rows // lanes, 2 * half, lanes), f32),
        ],
        compiler_params=pltpu.CompilerParams(vmem_limit_bytes=44 * 2**20),
        cost_estimate=pl.CostEstimate(
            flops=12 * rows * keys * width, bytes_accessed=8 * keys * width * 2, transcendentals=rows * keys
        ),
    )(live, own, oth)


def pack_kernel(chips, split, width, q_ref, k_ref, v_ref, g_ref, out_ref, held, sems):
    rows, columns = held.shape[1:]
    first = chips * width if split else 0
    copies = [
        pltpu.make_async_copy(ref.at[:, first : first + columns], held.at[n], sems.at[n])
        for n, ref in enumerate((q_ref, g_ref, k_ref, v_ref))
    ]
    for copy in copies:
        copy.start()
    for n, copy in enumerate(copies):
        copy.wait()
        for i in range(chips):
            if not split:
                out_ref[i, n] = held[n, :, i * width : (i + 1) * width]
                continue
            at = slice(i // 2 * width, (i // 2 + 1) * width)
            cut = slice(i % 2 * (rows // 2), (i % 2 + 1) * (rows // 2))
            if n < 2:
                out_ref[i, 0, n * (rows // 2) : (n + 1) * (rows // 2)] = held[n, cut, at]
            else:
                out_ref[i, n - 1] = held[n, :, at]


def pack_call(arrays, chips, split, width):
    rows, total = arrays[0].shape
    columns = total - chips * width if split else chips * width
    slots = 3 if split else 4
    return pl.pallas_call(
        functools.partial(pack_kernel, chips, split, width),
        out_shape=jax.ShapeDtypeStruct((chips, slots, rows, width), jnp.bfloat16),
        in_specs=[pl.BlockSpec(memory_space=pltpu.HBM)] * 4,
        out_specs=pl.BlockSpec(memory_space=pltpu.VMEM),
        scratch_shapes=[pltpu.VMEM((4, rows, columns), jnp.bfloat16), pltpu.SemaphoreType.DMA((4,))],
        compiler_params=pltpu.CompilerParams(vmem_limit_bytes=60 * 2**20),
    )(*arrays)


def unpack_kernel(chips, width, a_ref, b_ref, out_ref, query_ref, key_ref, value_ref, held, sems):
    rows = held.shape[1]
    copies = []
    for s, ref in enumerate((out_ref, query_ref, key_ref, value_ref)):
        for i in range(chips):
            held[s, :, i * width : (i + 1) * width] = a_ref[i, s]
        for i in range(chips // 2):
            at = slice((chips + i) * width, (chips + i + 1) * width)
            if s < 2:
                cut = slice(s * (rows // 2), (s + 1) * (rows // 2))
                for part in range(2):
                    held[s, part * (rows // 2) : (part + 1) * (rows // 2), at] = b_ref[2 * i + part, 0, cut]
            else:
                one = b_ref[2 * i, s - 1].astype(jnp.float32) + b_ref[2 * i + 1, s - 1].astype(jnp.float32)
                held[s, :, at] = one.astype(jnp.bfloat16)
        copies.append(pltpu.make_async_copy(held.at[s], ref, sems.at[s]))
        copies[-1].start()
    for copy in copies:
        copy.wait()


def unpack_call(back_a, back_b, heads):
    chips, _, rows, width = back_a.shape
    vm = pl.BlockSpec(memory_space=pltpu.VMEM)
    return pl.pallas_call(
        functools.partial(unpack_kernel, chips, width),
        out_shape=[jax.ShapeDtypeStruct((rows, heads * width), jnp.bfloat16)] * 4,
        in_specs=[vm, vm],
        out_specs=[pl.BlockSpec(memory_space=pltpu.HBM)] * 4,
        scratch_shapes=[pltpu.VMEM((4, rows, heads * width), jnp.bfloat16), pltpu.SemaphoreType.DMA((4,))],
        compiler_params=pltpu.CompilerParams(vmem_limit_bytes=16 * 2**20),
    )(back_a, back_b)


def after(array, *first):
    hbm = pl.BlockSpec(memory_space=pl.ANY)
    return pl.pallas_call(
        lambda *refs: None,
        out_shape=jax.ShapeDtypeStruct(array.shape, array.dtype),
        in_specs=[hbm] * (1 + len(first)),
        out_specs=hbm,
        input_output_aliases={0: 0},
        compiler_params=pltpu.CompilerParams(vmem_limit_bytes=2**20),
    )(array, *first)


def body(query, key_in, value, grad_out, masks):
    peers = lax.axis_size("seq")
    chips = peers // 2
    position = lax.axis_index("seq")
    chip, core = position // 2, position % 2
    heads, blocks = masks.shape[:2]
    width = query.shape[1] // heads
    tile = query.shape[0]
    groups = [list(range(e, peers, 2)) for e in range(2)]
    swap = [(i, i ^ 1) for i in range(peers)]

    def exchange(array):
        return lax.all_to_all(array, "seq", 0, 0, axis_index_groups=groups, tiled=True)

    def live_of(head):
        live = lax.dynamic_index_in_dim(masks, head, 0, keepdims=False).reshape(chips, 2, chips, 2)
        live = lax.dynamic_index_in_dim(live, core, 1, keepdims=False)
        live = jnp.where(core == 0, live, live[:, :, ::-1])
        return live.transpose(2, 1, 0).reshape(blocks, chips).astype(jnp.bfloat16)

    def gather(rows, give):
        taken = lax.ppermute(give, "seq", swap)
        total = rows[:, -2:].astype(jnp.float32) + taken.astype(jnp.float32)
        return rows.at[:, -2:].set(total.astype(jnp.bfloat16))

    arrays = (query, key_in, value, grad_out)
    live_b = live_of(chips + chip // 2)
    live_a = live_of(chip)
    got_b = exchange(pack_call(arrays, chips, True, width))
    got_a = exchange(after(pack_call(arrays, chips, False, width), live_a, live_b))
    other_b = lax.ppermute(got_b, "seq", swap)
    rows_b, give_b = attend_call(live_b, got_b, other_b, True)
    send_b = gather(rows_b, after(give_b, got_a))
    got_a = after(got_a, send_b)
    back_b = exchange(send_b)
    other_a = lax.ppermute(got_a, "seq", swap)
    rows_a, give_a = attend_call(live_a, got_a, other_a, False)
    back_a = exchange(gather(rows_a, after(give_a, back_b)))
    return tuple(unpack_call(back_a, back_b, heads))


def solution(mesh):
    tokens = P(("dp", "seq"), None)
    return jax.shard_map(
        body,
        mesh=mesh,
        in_specs=(tokens, tokens, tokens, tokens, P("dp", None, None)),
        out_specs=(tokens, tokens, tokens, tokens),
        check_vma=False,
    )
```

```python
import functools

import jax
import jax.numpy as jnp
from jax import lax
from jax.experimental import pallas as pl
from jax.experimental.pallas import tpu as pltpu
from jax.sharding import PartitionSpec as P

LANES = 512
BLOCK = 256
STEP = 2048
NT = (((1,), (1,)), ((), ()))
NN = (((1,), (0,)), ((), ()))
LOG2E = 1.4426950408889634


def at_multiple(x, n):
    return x if isinstance(x, int) else pl.multiple_of(x, n)


def dense_kernel(block, step_rows, lanes, split, masks_ref, own_ref, oth_ref, *refs):
    (rows_ref, give_ref,
    k_scr, v_scr, kt_scr, vt_scr, dk_scr, dv_scr, x_scr, p_scr, bias_ref, mask_scr, sem) = refs[-13:]
    half, slots, tile, width = own_ref.shape
    keys = 2 * half * tile
    queries = half * tile // (2 if split else 1)
    tiles = queries // lanes
    scale = width ** -0.5
    c2 = scale * LOG2E
    ks = slots - 2
    f32, bf16 = jnp.float32, jnp.bfloat16
    per = lanes // tile * (2 if split else 1)
    hr = lanes // per
    subs = step_rows // block
    tall = vt_scr.shape[0]

    def dot(a, b, dims=NN):
        return lax.dot_general(a, b, dims, preferred_element_type=f32)

    def prep(c, _):
        for src, base, s0 in ((own_ref, 0, ks), (oth_ref, half, oth_ref.shape[1] - 2)):
            k = src[c, s0]
            v = src[c, s0 + 1]
            at = pl.ds(pl.multiple_of((base + c) * tile, tile), tile)
            k_scr[at, :] = k
            v_scr[at, :] = v
            kt_scr[:, at] = k.T
            vt_scr[0:width, at] = v.T
            vt_scr[width:, at] = jnp.ones((tall - width, tile), bf16)
            dk_scr[at, :] = jnp.zeros((tile, width), f32)
            dv_scr[at, :] = jnp.zeros((tile, width), f32)
        return 0

    core = lax.axis_index("seq") % 2
    chip = lax.axis_index("seq") // 2
    head = half + chip // 2 if split else chip
    fetch = pltpu.make_async_copy(masks_ref.at[head], mask_scr, sem)
    fetch.start()
    lax.fori_loop(0, half, prep, 0)
    fetch.wait()
    blocks = 2 * half
    key = lax.broadcasted_iota(jnp.int32, (blocks, blocks), 0)
    from_block = lax.broadcasted_iota(jnp.int32, (blocks, blocks), 1)
    source = 2 * (key % half) + jnp.where(key < half, core, 1 - core)
    pick = (source == from_block).astype(f32).astype(bf16)
    seen = dot(pick, (mask_scr[...] > 0).astype(f32).astype(bf16), NT).astype(bf16)
    lane = lax.broadcasted_iota(jnp.int32, (blocks, lanes), 1)
    row = lax.broadcasted_iota(jnp.int32, (blocks, lanes), 0)
    for t in range(tiles):
        spread = (2 * (lane // hr + per * t) + core == row).astype(f32).astype(bf16)
        bias_ref[t] = jnp.where(dot(seen, spread) > 0.5, 0.0, -1e30)

    def q_tile(t):
        if split:
            return jnp.concatenate([own_ref[per * t + i, 0, :hr] for i in range(per)], 0)
        return jnp.concatenate([own_ref[per * t + i, 0] for i in range(per)], 0)

    def g_tile(t):
        if split:
            return jnp.concatenate([own_ref[per * t + i, 0, hr:] for i in range(per)], 0)
        return jnp.concatenate([own_ref[per * t + i, 1] for i in range(per)], 0)

    def put(t, slot, x):
        for i in range(per):
            part = x[i * hr : (i + 1) * hr].astype(bf16)
            if split:
                rows_ref[per * t + i, 0, slot * hr : (slot + 1) * hr] = part
            else:
                rows_ref[per * t + i, slot] = part

    def stage(t):
        scores, probs, grads = t + 1 < tiles, 0 <= t < tiles, 0 <= t - 1
        q_next = q_tile(t + 1) if scores else None
        if grads:
            g, (qn, gn, delta, _) = g_tile(t - 1), closed[t - 1]
        if probs:
            top = jnp.max(tops[t], axis=0, keepdims=True) * c2

        def step(i, carry):
            best, o, dq = carry
            at = pl.ds(at_multiple(i * step_rows, step_rows), step_rows)
            ds_all, p_all = [], []
            for u in range(subs):
                row = at_multiple(i * step_rows + u * block, block)
                sub = pl.ds(row, block)
                if grads:
                    pb = p_scr[sub, :]
                    dp = dot(v_scr[sub, :], g, NT)
                    ds = pb * (dp - delta).astype(bf16)
                    dv_scr[sub, :] += dot(pb, gn)
                    dk_scr[sub, :] += dot(ds, qn)
                    ds_all.append(ds)
                if probs:
                    pb = jnp.exp2(x_scr[sub, :] * c2 - top).astype(bf16)
                    p_scr[sub, :] = pb
                    p_all.append(pb)
                if scores:
                    s = dot(k_scr[sub, :], q_next, NT).reshape(block // tile, tile, lanes)
                    for w in range(block // tile):
                        x = s[w] + bias_ref[t + 1, pl.ds(i * (step_rows // tile) + u * (block // tile) + w, 1), :]
                        x_scr[pl.ds(at_multiple(row + w * tile, tile), tile), :] = x
                        best = jnp.maximum(best, jnp.max(x.reshape(tile // 8, 8, lanes), axis=0))
            if grads:
                dq = dq + dot(kt_scr[:, at], jnp.concatenate(ds_all, 0))
            if probs:
                o = o + dot(vt_scr[:, at], jnp.concatenate(p_all, 0))
            return best, o, dq

        start = (
            jnp.full((8, lanes), -1e30, f32) if scores else 0,
            jnp.zeros((tall, lanes), f32) if probs else 0,
            jnp.zeros((width, lanes), f32) if grads else 0,
        )
        best, o, dq = step(0, start) if keys == step_rows else lax.fori_loop(0, keys // step_rows, step, start)
        if scores:
            tops[t + 1] = best
        if grads:
            put(t - 1, 1, (dq * (closed[t - 1][3] * scale)).T)
        if probs:
            rl = 1.0 / o[width : width + 1]
            ot = o[:width] * rl
            put(t, 0, ot.T)
            gf = g_tile(t).astype(f32)
            delta = jnp.sum(gf.T * ot, axis=0, keepdims=True)
            column = jnp.broadcast_to(rl, (width, lanes)).T
            closed[t] = ((q_tile(t).astype(f32) * column).astype(bf16), (gf * column).astype(bf16), delta, rl)

    tops, closed = {}, {}
    for t in range(-1, tiles + 1):
        stage(t)

    def finish(c, _):
        for base, ref, slot in ((0, rows_ref, slots - 2), (half, give_ref, 0)):
            at = pl.ds(pl.multiple_of((base + c) * tile, tile), tile)
            ref[c, slot] = (dk_scr[at, :] * scale).astype(bf16)
            ref[c, slot + 1] = dv_scr[at, :].astype(bf16)
        return 0

    lax.fori_loop(0, half, finish, 0)


def attend_call(masks, own, oth, first, split):
    half, slots, tile, width = own.shape
    keys = 2 * half * tile
    rows = half * tile // (2 if split else 1)
    lanes = min(LANES, rows)
    f32, bf16 = jnp.float32, jnp.bfloat16
    vm = pl.BlockSpec(memory_space=pltpu.VMEM)
    any_ = pl.BlockSpec(memory_space=pl.ANY)
    return pl.pallas_call(
        functools.partial(dense_kernel, BLOCK, min(STEP, keys), lanes, split),
        out_shape=(
            jax.ShapeDtypeStruct((half, slots, tile, width), bf16),
            jax.ShapeDtypeStruct((half, 2, tile, width), bf16),
        ),
        in_specs=[any_, vm, vm] + [any_] * len(first),
        out_specs=[vm, vm],
        scratch_shapes=[
            pltpu.VMEM((keys, width), bf16),
            pltpu.VMEM((keys, width), bf16),
            pltpu.VMEM((width, keys), bf16),
            pltpu.VMEM((width + 16, keys), bf16),
            pltpu.VMEM((keys, width), f32),
            pltpu.VMEM((keys, width), f32),
            pltpu.VMEM((keys, lanes), f32),
            pltpu.VMEM((keys, lanes), bf16),
            pltpu.VMEM((rows // lanes, 2 * half, lanes), f32),
            pltpu.VMEM((2 * half, 2 * half), jnp.int32),
            pltpu.SemaphoreType.DMA(()),
        ],
        compiler_params=pltpu.CompilerParams(vmem_limit_bytes=36 * 2**20),
        cost_estimate=pl.CostEstimate(
            flops=12 * rows * keys * width, bytes_accessed=8 * keys * width * 2, transcendentals=rows * keys
        ),
    )(masks, own, oth, *first)


def pack_kernel(chips, width, q_ref, k_ref, v_ref, g_ref, a_ref, b_ref, held, a_scr, b_scr, in_sems, out_sems):
    rows, total = held.shape[1:]
    hr = rows // 2
    copies = [
        pltpu.make_async_copy(ref, held.at[n], in_sems.at[n]) for n, ref in enumerate((q_ref, g_ref, k_ref, v_ref))
    ]
    for copy in copies:
        copy.start()
    sends = []
    for n, copy in enumerate(copies):
        copy.wait()
        for i in range(chips):
            a_scr[i, n] = held[n, :, i * width : (i + 1) * width]
            at = slice((chips + i // 2) * width, (chips + i // 2 + 1) * width)
            if n < 2:
                b_scr[i, 0, n * hr : (n + 1) * hr] = held[n, i % 2 * hr : (i % 2 + 1) * hr, at]
            else:
                b_scr[i, n - 1] = held[n, :, at]
        sends.append(pltpu.make_async_copy(a_scr.at[:, n], a_ref.at[:, n], out_sems.at[n]))
        if n > 0:
            sends.append(pltpu.make_async_copy(b_scr.at[:, n - 1], b_ref.at[:, n - 1], out_sems.at[3 + n]))
        for send in sends[-2 if n else -1 :]:
            send.start()
    for send in sends:
        send.wait()


def pack_call(arrays, chips, width):
    rows, total = arrays[0].shape
    bf16 = jnp.bfloat16
    hbm = pl.BlockSpec(memory_space=pltpu.HBM)
    shapes = [(chips, slots, rows, width) for slots in (4, 3)]
    return pl.pallas_call(
        functools.partial(pack_kernel, chips, width),
        out_shape=[jax.ShapeDtypeStruct(shape, bf16) for shape in shapes],
        in_specs=[hbm] * 4,
        out_specs=[hbm] * 2,
        scratch_shapes=[pltpu.VMEM((4, rows, total), bf16)]
        + [pltpu.VMEM(shape, bf16) for shape in shapes]
        + [pltpu.SemaphoreType.DMA((4,)), pltpu.SemaphoreType.DMA((7,))],
        compiler_params=pltpu.CompilerParams(vmem_limit_bytes=60 * 2**20),
    )(*arrays)


def unpack_kernel(chips, width, a_ref, b_ref, out_ref, query_ref, key_ref, value_ref, held, sems):
    rows = held.shape[1]
    copies = []
    for s, ref in enumerate((out_ref, query_ref, key_ref, value_ref)):
        for i in range(chips):
            held[s, :, i * width : (i + 1) * width] = a_ref[i, s]
        for i in range(chips // 2):
            at = slice((chips + i) * width, (chips + i + 1) * width)
            if s < 2:
                cut = slice(s * (rows // 2), (s + 1) * (rows // 2))
                for part in range(2):
                    held[s, part * (rows // 2) : (part + 1) * (rows // 2), at] = b_ref[2 * i + part, 0, cut]
            else:
                one = b_ref[2 * i, s - 1].astype(jnp.float32) + b_ref[2 * i + 1, s - 1].astype(jnp.float32)
                held[s, :, at] = one.astype(jnp.bfloat16)
        copies.append(pltpu.make_async_copy(held.at[s], ref, sems.at[s]))
        copies[-1].start()
    for copy in copies:
        copy.wait()


def unpack_call(back_a, back_b, heads):
    chips, _, rows, width = back_a.shape
    vm = pl.BlockSpec(memory_space=pltpu.VMEM)
    return pl.pallas_call(
        functools.partial(unpack_kernel, chips, width),
        out_shape=[jax.ShapeDtypeStruct((rows, heads * width), jnp.bfloat16)] * 4,
        in_specs=[vm, vm],
        out_specs=[pl.BlockSpec(memory_space=pltpu.HBM)] * 4,
        scratch_shapes=[pltpu.VMEM((4, rows, heads * width), jnp.bfloat16), pltpu.SemaphoreType.DMA((4,))],
        compiler_params=pltpu.CompilerParams(vmem_limit_bytes=16 * 2**20),
    )(back_a, back_b)


def after(array, *first):
    hbm = pl.BlockSpec(memory_space=pl.ANY)
    return pl.pallas_call(
        lambda *refs: None,
        out_shape=jax.ShapeDtypeStruct(array.shape, array.dtype),
        in_specs=[hbm] * (1 + len(first)),
        out_specs=hbm,
        input_output_aliases={0: 0},
        compiler_params=pltpu.CompilerParams(vmem_limit_bytes=2**20),
    )(array, *first)


def body(query, key_in, value, grad_out, masks):
    peers = lax.axis_size("seq")
    chips = peers // 2
    heads = masks.shape[0]
    width = query.shape[1] // heads
    groups = [list(range(e, peers, 2)) for e in range(2)]
    swap = [(i, i ^ 1) for i in range(peers)]

    def exchange(array):
        return lax.all_to_all(array, "seq", 0, 0, axis_index_groups=groups, tiled=True)

    def gather(rows, give):
        taken = lax.ppermute(give, "seq", swap)
        total = rows[:, -2:].astype(jnp.float32) + taken.astype(jnp.float32)
        return rows.at[:, -2:].set(total.astype(jnp.bfloat16))

    arrays = (query, key_in, value, grad_out)
    send_a, send_b = pack_call(arrays, chips, width)
    got_a = exchange(send_a)
    got_b = exchange(send_b)
    other_a = lax.ppermute(got_a, "seq", swap)
    rows_a, give_a = attend_call(masks, got_a, other_a, (), False)
    back_a = gather(rows_a, after(give_a, got_b))
    other_b = lax.ppermute(got_b, "seq", swap)
    rows_b, give_b = attend_call(masks, got_b, other_b, (back_a,), True)
    back_a = exchange(back_a)
    back_b = exchange(gather(rows_b, after(give_b, back_a)))
    return tuple(unpack_call(back_a, back_b, heads))


def solution(mesh):
    tokens = P(("dp", "seq"), None)
    return jax.shard_map(
        body,
        mesh=mesh,
        in_specs=(tokens, tokens, tokens, tokens, P("dp", None, None)),
        out_specs=(tokens, tokens, tokens, tokens),
        check_vma=False,
    )
```

```python
import functools

import jax
import jax.numpy as jnp
from jax import lax
from jax.experimental import pallas as pl
from jax.experimental.pallas import tpu as pltpu
from jax.sharding import PartitionSpec as P

LANES = 512
BLOCK = 512
STEPS_WHOLE = (4096, 4096, 4096, 4096, 4096)
STEPS_SPLIT = (512, 512, 512, 512, 512)
NT = (((1,), (1,)), ((), ()))
NN = (((1,), (0,)), ((), ()))
LOG2E = 1.4426950408889634


def at_multiple(x, n):
    return x if isinstance(x, int) else pl.multiple_of(x, n)


def attend_kernel(
    steps, lanes, split, depends, masks_ref, own_ref, oth_ref, *refs
):
    send_ref, keep_ref, give_ref = refs[depends : depends + 3]
    (rows_scr, qg_scr, k_scr, v_scr, kt_scr, vt_scr, dk_scr, dv_scr, x_scr, p_scr, bias_scr, mask_scr) = refs[depends + 3 : depends + 15]
    (top_scr, qn_scr, gn_scr, stat_scr, give_scr, keep_scr, sems) = refs[depends + 15 :]
    half, slots, tile, width = own_ref.shape
    blocks = 2 * half
    keys = blocks * tile
    queries = half * tile // (2 if split else 1)
    tiles = queries // lanes
    scale = width ** -0.5
    c2 = scale * LOG2E
    ks = slots - 2
    f32, bf16 = jnp.float32, jnp.bfloat16
    per = lanes // tile * (2 if split else 1)
    hr = lanes // per
    tall = vt_scr.shape[0]

    def dot(a, b, dims=NN):
        return lax.dot_general(a, b, dims, preferred_element_type=f32)

    core = lax.axis_index("seq") % 2
    chip = lax.axis_index("seq") // 2
    head = half + chip // 2 if split else chip
    copies = [
        pltpu.make_async_copy(masks_ref.at[head], mask_scr, sems.at[0]),
        pltpu.make_async_copy(own_ref.at[:, ks], k_scr.at[0:half], sems.at[1]),
        pltpu.make_async_copy(oth_ref.at[:, ks], k_scr.at[half:blocks], sems.at[2]),
        pltpu.make_async_copy(own_ref.at[:, 0:ks], qg_scr, sems.at[3]),
        pltpu.make_async_copy(own_ref.at[:, ks + 1], v_scr.at[0:half], sems.at[4]),
        pltpu.make_async_copy(oth_ref.at[:, ks + 1], v_scr.at[half:blocks], sems.at[5]),
    ]
    for copy in copies:
        copy.start()
    copies[0].wait()

    key = lax.broadcasted_iota(jnp.int32, (blocks, blocks), 0)
    from_block = lax.broadcasted_iota(jnp.int32, (blocks, blocks), 1)
    source = 2 * (key % half) + jnp.where(key < half, core, 1 - core)
    pick = (source == from_block).astype(f32).astype(bf16)
    seen = dot(pick, (mask_scr[...] > 0).astype(f32).astype(bf16), NT).astype(bf16)
    lane = lax.broadcasted_iota(jnp.int32, (blocks, lanes), 1)
    row = lax.broadcasted_iota(jnp.int32, (blocks, lanes), 0)
    for t in range(tiles):
        spread = (2 * (lane // hr + per * t) + core == row).astype(f32).astype(bf16)
        bias_scr[t] = jnp.where(dot(seen, spread) > 0.5, 0.0, -1e30)
    for copy in copies[1:]:
        copy.wait()

    def q_tile(t):
        if split:
            return jnp.concatenate([qg_scr[per * t + i, 0, :hr] for i in range(per)], 0)
        return jnp.concatenate([qg_scr[per * t + i, 0] for i in range(per)], 0)

    def g_tile(t):
        if split:
            return jnp.concatenate([qg_scr[per * t + i, 0, hr:] for i in range(per)], 0)
        return jnp.concatenate([qg_scr[per * t + i, 1] for i in range(per)], 0)

    def put(t, slot, x):
        for i in range(per):
            part = x[i * hr : (i + 1) * hr].astype(bf16)
            if split:
                rows_scr[per * t + i, 0, slot * hr : (slot + 1) * hr] = part
            else:
                rows_scr[per * t + i, slot] = part

    def stage(t, scores, probs, grads, step_rows):
        prepare = not probs and not grads
        subs = step_rows // BLOCK
        if scores:
            q_next = q_tile(t + 1)
        if grads:
            g, qn, gn = g_tile(t - 1), qn_scr[...], gn_scr[...]
            delta, rl_last = stat_scr[0:1, :], stat_scr[1:2, :]
        if probs:
            top = jnp.max(top_scr[...], axis=0, keepdims=True) * c2

        def step(i, carry):
            best, o, dq = carry
            at = pl.ds(at_multiple(i * step_rows, step_rows), step_rows)
            ds_all, p_all = [], []
            for u in range(subs):
                first = i * step_rows + u * BLOCK
                sub = pl.ds(at_multiple(first, BLOCK), BLOCK)
                pair = pl.ds(i * (step_rows // tile) + u * (BLOCK // tile), BLOCK // tile)
                if grads:
                    pb = p_scr[sub, :]
                    dp = dot(v_scr[pair].reshape(BLOCK, width), g, NT)
                    ds = pb * (dp - delta).astype(bf16)
                    dv_scr[sub, :] += dot(pb, gn)
                    dk_scr[sub, :] += dot(ds, qn)
                    ds_all.append(ds)
                if probs:
                    pb = jnp.exp2(x_scr[sub, :] * c2 - top).astype(bf16)
                    p_scr[sub, :] = pb
                    p_all.append(pb)
                if scores:
                    s = dot(k_scr[pair].reshape(BLOCK, width), q_next, NT).reshape(BLOCK // tile, tile, lanes)
                    for w in range(BLOCK // tile):
                        x = s[w] + bias_scr[t + 1, pl.ds(i * (step_rows // tile) + u * (BLOCK // tile) + w, 1), :]
                        x_scr[pl.ds(at_multiple(first + w * tile, tile), tile), :] = x
                        best = jnp.maximum(best, jnp.max(x.reshape(tile // 8, 8, lanes), axis=0))
                if prepare:
                    for w in range(BLOCK // tile):
                        j = i * (step_rows // tile) + u * (BLOCK // tile) + w
                        to = pl.ds(at_multiple(first + w * tile, tile), tile)
                        kt_scr[:, to] = k_scr[j].T
                        vt_scr[0:width, to] = v_scr[j].T
                        vt_scr[width:, to] = jnp.ones((tall - width, tile), bf16)
                        dk_scr[to, :] = jnp.zeros((tile, width), f32)
                        dv_scr[to, :] = jnp.zeros((tile, width), f32)
            if grads:
                dq = dq + dot(kt_scr[:, at], jnp.concatenate(ds_all, 0))
            if probs:
                o = o + dot(vt_scr[:, at], jnp.concatenate(p_all, 0))
            return best, o, dq

        start = (
            jnp.full((8, lanes), -1e30, f32) if scores else 0,
            jnp.zeros((tall, lanes), f32) if probs else 0,
            jnp.zeros((width, lanes), f32) if grads else 0,
        )
        if keys == step_rows:
            best, o, dq = step(0, start)
        else:
            best, o, dq = lax.fori_loop(0, keys // step_rows, step, start)
        if scores:
            top_scr[...] = best
        if grads:
            put(t - 1, 1, (dq * (rl_last * scale)).T)
        if probs:
            rl = 1.0 / o[width : width + 1]
            ot = o[:width] * rl
            put(t, 0, ot.T)
            gf = g_tile(t).astype(f32)
            stat_scr[0:1, :] = jnp.sum(gf.T * ot, axis=0, keepdims=True)
            stat_scr[1:2, :] = rl
            column = jnp.broadcast_to(rl, (width, lanes)).T
            qn_scr[...] = (q_tile(t).astype(f32) * column).astype(bf16)
            gn_scr[...] = (gf * column).astype(bf16)

    stage(-1, True, False, False, steps[0])
    stage(0, True, True, False, steps[1])

    if tiles > 2:

        def middle(t, _):
            stage(t, True, True, True, steps[2])
            return 0

        lax.fori_loop(1, tiles - 1, middle, 0)
    stage(tiles - 1, False, True, True, steps[3])
    stage(tiles, False, False, True, steps[4])
    rows_out = pltpu.make_async_copy(rows_scr, send_ref.at[:, 0:ks], sems.at[0])
    rows_out.start()

    def finish(base, ref):
        def copy(c, _):
            at = pl.ds(pl.multiple_of((base + c) * tile, tile), tile)
            ref[c, 0] = (dk_scr[at, :] * scale).astype(bf16)
            ref[c, 1] = dv_scr[at, :].astype(bf16)
            return 0

        lax.fori_loop(0, half, copy, 0)

    finish(half, give_scr)
    give_out = pltpu.make_async_copy(give_scr, give_ref, sems.at[1])
    give_out.start()
    finish(0, keep_scr)
    keep_out = pltpu.make_async_copy(keep_scr, keep_ref, sems.at[2])
    keep_out.start()
    rows_out.wait()
    give_out.wait()
    keep_out.wait()


def attend_call(masks, own, oth, depends, split):
    half, slots, tile, width = own.shape
    keys = 2 * half * tile
    rows = half * tile // (2 if split else 1)
    lanes = min(LANES, rows // 2)
    f32, bf16 = jnp.float32, jnp.bfloat16
    any_ = pl.BlockSpec(memory_space=pl.ANY)
    hbm = pl.BlockSpec(memory_space=pltpu.HBM)
    return pl.pallas_call(
        functools.partial(attend_kernel, STEPS_SPLIT if split else STEPS_WHOLE, lanes, split, len(depends)),
        out_shape=(
            jax.ShapeDtypeStruct((half, slots, tile, width), bf16),
            jax.ShapeDtypeStruct((half, 2, tile, width), bf16),
            jax.ShapeDtypeStruct((half, 2, tile, width), bf16),
        ),
        in_specs=[any_] * (3 + len(depends)),
        out_specs=[hbm, hbm, hbm],
        scratch_shapes=[
            pltpu.VMEM((half, slots - 2, tile, width), bf16),
            pltpu.VMEM((half, slots - 2, tile, width), bf16),
            pltpu.VMEM((2 * half, tile, width), bf16),
            pltpu.VMEM((2 * half, tile, width), bf16),
            pltpu.VMEM((width, keys), bf16),
            pltpu.VMEM((width + 16, keys), bf16),
            pltpu.VMEM((keys, width), f32),
            pltpu.VMEM((keys, width), f32),
            pltpu.VMEM((keys, lanes), f32),
            pltpu.VMEM((keys, lanes), bf16),
            pltpu.VMEM((rows // lanes, 2 * half, lanes), f32),
            pltpu.VMEM((2 * half, 2 * half), jnp.int32),
            pltpu.VMEM((8, lanes), f32),
            pltpu.VMEM((lanes, width), bf16),
            pltpu.VMEM((lanes, width), bf16),
            pltpu.VMEM((8, lanes), f32),
            pltpu.VMEM((half, 2, tile, width), bf16),
            pltpu.VMEM((half, 2, tile, width), bf16),
            pltpu.SemaphoreType.DMA((6,)),
        ],
        compiler_params=pltpu.CompilerParams(vmem_limit_bytes=(251 if split else 248) * 2**18),
        cost_estimate=pl.CostEstimate(
            flops=12 * rows * keys * width, bytes_accessed=8 * keys * width * 2, transcendentals=rows * keys
        ),
    )(masks, own, oth, *depends)


def join_kernel(rows_ref, keep_ref, taken_ref, *refs):
    send_ref, keep_scr, taken_scr, sum_scr, sems = refs[-5:]
    chips, slots = send_ref.shape[:2]
    parts = sems.shape[1]
    cuts = [pl.ds(n * (chips // parts), chips // parts) for n in range(parts)]
    loads = [
        pltpu.make_async_copy(ref.at[cut], scr.at[cut], sems.at[k, n])
        for n, cut in enumerate(cuts)
        for k, (ref, scr) in enumerate(((keep_ref, keep_scr), (taken_ref, taken_scr)))
    ]
    stores = [
        pltpu.make_async_copy(sum_scr.at[cut], send_ref.at[cut, slots - 2 : slots], sems.at[2, n])
        for n, cut in enumerate(cuts)
    ]
    for load in loads:
        load.start()
    for n in range(parts):
        loads[2 * n].wait()
        loads[2 * n + 1].wait()

        def add(c, _):
            for s in range(2):
                total = keep_scr[c, s].astype(jnp.float32) + taken_scr[c, s].astype(jnp.float32)
                sum_scr[c, s] = total.astype(jnp.bfloat16)
            return 0

        lax.fori_loop(n * (chips // parts), (n + 1) * (chips // parts), add, 0)
        stores[n].start()
    for store in stores:
        store.wait()


def join_call(rows, keep, taken, depends, grant):
    hbm = pl.BlockSpec(memory_space=pltpu.HBM)
    return pl.pallas_call(
        join_kernel,
        out_shape=jax.ShapeDtypeStruct(rows.shape, rows.dtype),
        in_specs=[hbm] + [pl.BlockSpec(memory_space=pl.ANY)] * (2 + len(depends)),
        out_specs=hbm,
        scratch_shapes=[pltpu.VMEM(keep.shape, keep.dtype)] * 3 + [pltpu.SemaphoreType.DMA((3, 4))],
        input_output_aliases={0: 0},
        compiler_params=pltpu.CompilerParams(vmem_limit_bytes=grant),
    )(rows, keep, taken, *depends)


def pack_kernel(chips, width, q_ref, k_ref, v_ref, g_ref, a_ref, b_ref, held, a_scr, b_scr, in_sems, out_sems):
    rows, total = held.shape[1:]
    hr = rows // 2
    copies = [
        pltpu.make_async_copy(ref, held.at[n], in_sems.at[n]) for n, ref in enumerate((q_ref, g_ref, k_ref, v_ref))
    ]
    for copy in copies:
        copy.start()
    sends = []
    for n, copy in enumerate(copies):
        copy.wait()
        for i in range(chips):
            a_scr[i, n] = held[n, :, i * width : (i + 1) * width]
            at = slice((chips + i // 2) * width, (chips + i // 2 + 1) * width)
            if n < 2:
                b_scr[i, 0, n * hr : (n + 1) * hr] = held[n, i % 2 * hr : (i % 2 + 1) * hr, at]
            else:
                b_scr[i, n - 1] = held[n, :, at]
        sends.append(pltpu.make_async_copy(a_scr.at[:, n], a_ref.at[:, n], out_sems.at[n]))
        if n > 0:
            sends.append(pltpu.make_async_copy(b_scr.at[:, n - 1], b_ref.at[:, n - 1], out_sems.at[3 + n]))
        for send in sends[-2 if n else -1 :]:
            send.start()
    for send in sends:
        send.wait()


def pack_call(arrays, chips, width):
    rows, total = arrays[0].shape
    bf16 = jnp.bfloat16
    hbm = pl.BlockSpec(memory_space=pltpu.HBM)
    shapes = [(chips, slots, rows, width) for slots in (4, 3)]
    return pl.pallas_call(
        functools.partial(pack_kernel, chips, width),
        out_shape=[jax.ShapeDtypeStruct(shape, bf16) for shape in shapes],
        in_specs=[hbm] * 4,
        out_specs=[hbm] * 2,
        scratch_shapes=[pltpu.VMEM((4, rows, total), bf16)]
        + [pltpu.VMEM(shape, bf16) for shape in shapes]
        + [pltpu.SemaphoreType.DMA((4,)), pltpu.SemaphoreType.DMA((7,))],
        compiler_params=pltpu.CompilerParams(vmem_limit_bytes=248 * 2**18),
    )(*arrays)


def unpack_whole(width, a_ref, out_ref, query_ref, key_ref, value_ref, got, held, in_sems, out_sems):
    chips = got.shape[1]
    loads = [pltpu.make_async_copy(a_ref.at[:, s], got.at[s], in_sems.at[s]) for s in range(4)]
    for load in loads:
        load.start()
    stores = []
    for s, ref in enumerate((out_ref, query_ref, key_ref, value_ref)):
        loads[s].wait()
        for i in range(chips):
            held[s, :, i * width : (i + 1) * width] = got[s, i]
        stores.append(pltpu.make_async_copy(held.at[s], ref.at[:, 0 : chips * width], out_sems.at[s]))
        stores[s].start()
    for store in stores:
        store.wait()


def unpack_split(width, b_ref, *refs):
    outs, (held, sems) = refs[4:8], refs[8:]
    chips, _, rows, _ = b_ref.shape
    hr = rows // 2
    stores = []
    for s, ref in enumerate(outs):
        for i in range(chips // 2):
            at = slice(i * width, (i + 1) * width)
            if s < 2:
                for part in range(2):
                    held[s, part * hr : (part + 1) * hr, at] = b_ref[2 * i + part, 0, s * hr : (s + 1) * hr]
            else:
                one = b_ref[2 * i, s - 1].astype(jnp.float32) + b_ref[2 * i + 1, s - 1].astype(jnp.float32)
                held[s, :, at] = one.astype(jnp.bfloat16)
        to = ref.at[:, chips * width : chips * width + held.shape[2]]
        stores.append(pltpu.make_async_copy(held.at[s], to, sems.at[s]))
        stores[s].start()
    for store in stores:
        store.wait()


def unpack_call(back_a, back_b, heads):
    chips, _, rows, width = back_a.shape
    bf16 = jnp.bfloat16
    hbm = pl.BlockSpec(memory_space=pltpu.HBM)
    any_ = pl.BlockSpec(memory_space=pl.ANY)
    shapes = [jax.ShapeDtypeStruct((rows, heads * width), bf16)] * 4
    sems = [pltpu.SemaphoreType.DMA((4,)), pltpu.SemaphoreType.DMA((4,))]
    params = pltpu.CompilerParams(vmem_limit_bytes=16 * 2**20)
    whole = pl.pallas_call(
        functools.partial(unpack_whole, width),
        out_shape=shapes,
        in_specs=[any_],
        out_specs=[hbm] * 4,
        scratch_shapes=[pltpu.VMEM((4, chips, rows, width), bf16), pltpu.VMEM((4, rows, chips * width), bf16)] + sems,
        compiler_params=params,
    )(back_a)
    return pl.pallas_call(
        functools.partial(unpack_split, width),
        out_shape=shapes,
        in_specs=[pl.BlockSpec(memory_space=pltpu.VMEM)] + [hbm] * 4,
        out_specs=[hbm] * 4,
        scratch_shapes=[pltpu.VMEM((4, rows, (heads - chips) * width), bf16), pltpu.SemaphoreType.DMA((4,))],
        input_output_aliases={1: 0, 2: 1, 3: 2, 4: 3},
        compiler_params=params,
    )(back_b, *whole)


def after(array, *first):
    hbm = pl.BlockSpec(memory_space=pl.ANY)
    return pl.pallas_call(
        lambda *refs: None,
        out_shape=jax.ShapeDtypeStruct(array.shape, array.dtype),
        in_specs=[hbm] * (1 + len(first)),
        out_specs=hbm,
        input_output_aliases={0: 0},
        compiler_params=pltpu.CompilerParams(vmem_limit_bytes=248 * 2**18),
    )(array, *first)


def body(query, key_in, value, grad_out, masks):
    peers = lax.axis_size("seq")
    chips = peers // 2
    heads = masks.shape[0]
    width = query.shape[1] // heads
    groups = [list(range(e, peers, 2)) for e in range(2)]
    swap = [(i, i ^ 1) for i in range(peers)]

    def exchange(array):
        return lax.all_to_all(array, "seq", 0, 0, axis_index_groups=groups, tiled=True)

    def gather(parts, first, grant):
        rows, keep, give = parts
        return join_call(rows, keep, lax.ppermute(give, "seq", swap), (first,), grant)

    arrays = (query, key_in, value, grad_out)
    send_a, send_b = pack_call(arrays, chips, width)
    got_a = exchange(send_a)
    got_b = exchange(send_b)
    other_a = lax.ppermute(got_a, "seq", swap)
    send_a = gather(attend_call(masks, got_a, other_a, (), False), got_b, 62 * 2**20)
    got_b = after(got_b, send_a)
    other_b = lax.ppermute(got_b, "seq", swap)
    parts_b = attend_call(masks, got_b, other_b, (), True)
    back_a = exchange(send_a)
    back_b = exchange(gather(parts_b, back_a, 56 * 2**20))
    return tuple(unpack_call(back_a, back_b, heads))


def solution(mesh):
    tokens = P(("dp", "seq"), None)
    return jax.shard_map(
        body,
        mesh=mesh,
        in_specs=(tokens, tokens, tokens, tokens, P("dp", None, None)),
        out_specs=(tokens, tokens, tokens, tokens),
        check_vma=False,
    )
```

```python
import functools

import jax
import jax.numpy as jnp
from jax import lax
from jax.experimental import pallas as pl
from jax.experimental.pallas import tpu as pltpu
from jax.sharding import PartitionSpec as P

LANES = 512
BLOCK = 512
GROUP = 4096
STEPS_WHOLE = (4096, 4096, 4096, 4096, 4096)
STEPS_SPLIT = (512, 512, 512, 512, 512)
NT = (((1,), (1,)), ((), ()))
NN = (((1,), (0,)), ((), ()))
LOG2E = 1.4426950408889634


def at_multiple(x, n):
    return x if isinstance(x, int) else pl.multiple_of(x, n)


def attend_kernel(
    steps, lanes, split, depends, masks_ref, own_ref, oth_ref, *refs
):
    send_ref, keep_ref, give_ref = refs[depends : depends + 3]
    (rows_scr, qg_scr, k_scr, v_scr, kt_scr, vt_scr, dk_scr, dv_scr, x_scr, p_scr, bias_scr, mask_scr) = refs[depends + 3 : depends + 15]
    (top_scr, stat_scr, give_scr, keep_scr, sems) = refs[depends + 15 :]
    half, slots, tile, width = own_ref.shape
    blocks = 2 * half
    keys = blocks * tile
    queries = half * tile // (2 if split else 1)
    tiles = queries // lanes
    scale = width ** -0.5
    c2 = scale * LOG2E
    ks = slots - 2
    f32, bf16 = jnp.float32, jnp.bfloat16
    per = lanes // tile * (2 if split else 1)
    hr = lanes // per
    tall = vt_scr.shape[0]

    def dot(a, b, dims=NN):
        return lax.dot_general(a, b, dims, preferred_element_type=f32)

    core = lax.axis_index("seq") % 2
    chip = lax.axis_index("seq") // 2
    head = half + chip // 2 if split else chip
    copies = [
        pltpu.make_async_copy(masks_ref.at[head], mask_scr, sems.at[0]),
        pltpu.make_async_copy(own_ref.at[:, ks], k_scr.at[0:half], sems.at[1]),
        pltpu.make_async_copy(oth_ref.at[:, ks], k_scr.at[half:blocks], sems.at[2]),
        pltpu.make_async_copy(own_ref.at[:, 0:ks], qg_scr, sems.at[3]),
        pltpu.make_async_copy(own_ref.at[:, ks + 1], v_scr.at[0:half], sems.at[4]),
        pltpu.make_async_copy(oth_ref.at[:, ks + 1], v_scr.at[half:blocks], sems.at[5]),
    ]
    for copy in copies:
        copy.start()
    copies[0].wait()

    key = lax.broadcasted_iota(jnp.int32, (blocks, blocks), 0)
    from_block = lax.broadcasted_iota(jnp.int32, (blocks, blocks), 1)
    source = 2 * (key % half) + jnp.where(key < half, core, 1 - core)
    pick = (source == from_block).astype(f32).astype(bf16)
    seen = dot(pick, (mask_scr[...] > 0).astype(f32).astype(bf16), NT).astype(bf16)
    lane = lax.broadcasted_iota(jnp.int32, (blocks, lanes), 1)
    row = lax.broadcasted_iota(jnp.int32, (blocks, lanes), 0)
    for t in range(tiles):
        spread = (2 * (lane // hr + per * t) + core == row).astype(f32).astype(bf16)
        bias_scr[t] = jnp.where(dot(seen, spread) > 0.5, 0.0, -1e30)
    for copy in copies[1:]:
        copy.wait()

    def q_tile(t):
        if split:
            return jnp.concatenate([qg_scr[per * t + i, 0, :hr] for i in range(per)], 0)
        return jnp.concatenate([qg_scr[per * t + i, 0] for i in range(per)], 0)

    def g_tile(t):
        if split:
            return jnp.concatenate([qg_scr[per * t + i, 0, hr:] for i in range(per)], 0)
        return jnp.concatenate([qg_scr[per * t + i, 1] for i in range(per)], 0)

    def put(t, slot, x):
        for i in range(per):
            part = x[i * hr : (i + 1) * hr].astype(bf16)
            if split:
                rows_scr[per * t + i, 0, slot * hr : (slot + 1) * hr] = part
            else:
                rows_scr[per * t + i, slot] = part

    def stage(t, scores, probs, grads, step_rows):
        prepare = not probs and not grads
        subs = step_rows // BLOCK
        if scores:
            q_next = q_tile(t + 1)
        if grads:
            g, q = g_tile(t - 1), q_tile(t - 1)
            delta, inverse = stat_scr[0:1, :], stat_scr[1:2, :].astype(bf16)
        if probs:
            top = jnp.max(top_scr[...], axis=0, keepdims=True) * c2

        def step(i, carry):
            best, o, dq = carry
            group = min(GROUP, step_rows)
            ds_all = []
            for u in range(subs):
                first = i * step_rows + u * BLOCK
                sub = pl.ds(at_multiple(first, BLOCK), BLOCK)
                pair = pl.ds(i * (step_rows // tile) + u * (BLOCK // tile), BLOCK // tile)
                if grads:
                    pb = p_scr[sub, :] * inverse
                    dp = dot(v_scr[pair].reshape(BLOCK, width), g, NT)
                    ds = pb * (dp - delta).astype(bf16)
                    dv_scr[sub, :] += dot(pb, g)
                    dk_scr[sub, :] += dot(ds, q)
                    ds_all.append(ds)
                if probs:
                    pb = jnp.exp2(x_scr[sub, :] * c2 - top).astype(bf16)
                    p_scr[sub, :] = pb
                if scores:
                    s = dot(k_scr[pair].reshape(BLOCK, width), q_next, NT).reshape(BLOCK // tile, tile, lanes)
                    for w in range(BLOCK // tile):
                        x = s[w] + bias_scr[t + 1, pl.ds(i * (step_rows // tile) + u * (BLOCK // tile) + w, 1), :]
                        x_scr[pl.ds(at_multiple(first + w * tile, tile), tile), :] = x
                        best = jnp.maximum(best, jnp.max(x.reshape(tile // 8, 8, lanes), axis=0))
                if prepare:
                    for w in range(BLOCK // tile):
                        j = i * (step_rows // tile) + u * (BLOCK // tile) + w
                        to = pl.ds(at_multiple(first + w * tile, tile), tile)
                        kt_scr[:, to] = k_scr[j].T
                        vt_scr[0:width, to] = v_scr[j].T
                        vt_scr[width:, to] = jnp.ones((tall - width, tile), bf16)
                        dk_scr[to, :] = jnp.zeros((tile, width), f32)
                        dv_scr[to, :] = jnp.zeros((tile, width), f32)
                if (u + 1) * BLOCK % group == 0:
                    at = pl.ds(at_multiple(first + BLOCK - group, group), group)
                    if grads:
                        dq = dq + dot(kt_scr[:, at], jnp.concatenate(ds_all, 0))
                        ds_all = []
                    if probs:
                        o = o + dot(vt_scr[:, at], p_scr[at, :])
            return best, o, dq

        start = (
            jnp.full((8, lanes), -1e30, f32) if scores else 0,
            jnp.zeros((tall, lanes), f32) if probs else 0,
            jnp.zeros((width, lanes), f32) if grads else 0,
        )
        if keys == step_rows:
            best, o, dq = step(0, start)
        else:
            best, o, dq = lax.fori_loop(0, keys // step_rows, step, start)
        if scores:
            top_scr[...] = best
        if grads:
            put(t - 1, 1, (dq * scale).T)
        if probs:
            rl = 1.0 / o[width : width + 1]
            ot = o[:width] * rl
            put(t, 0, ot.T)
            gf = g_tile(t).astype(f32)
            stat_scr[0:1, :] = jnp.sum(gf.T * ot, axis=0, keepdims=True)
            stat_scr[1:2, :] = rl

    stage(-1, True, False, False, steps[0])
    stage(0, True, True, False, steps[1])

    if tiles > 2:

        def middle(t, _):
            stage(t, True, True, True, steps[2])
            return 0

        lax.fori_loop(1, tiles - 1, middle, 0)
    stage(tiles - 1, False, True, True, steps[3])
    stage(tiles, False, False, True, steps[4])
    rows_out = pltpu.make_async_copy(rows_scr, send_ref.at[:, 0:ks], sems.at[0])
    rows_out.start()

    def finish(base, ref):
        def copy(c, _):
            at = pl.ds(pl.multiple_of((base + c) * tile, tile), tile)
            ref[c, 0] = (dk_scr[at, :] * scale).astype(bf16)
            ref[c, 1] = dv_scr[at, :].astype(bf16)
            return 0

        lax.fori_loop(0, half, copy, 0)

    finish(half, give_scr)
    give_out = pltpu.make_async_copy(give_scr, give_ref, sems.at[1])
    give_out.start()
    finish(0, keep_scr)
    keep_out = pltpu.make_async_copy(keep_scr, keep_ref, sems.at[2])
    keep_out.start()
    rows_out.wait()
    give_out.wait()
    keep_out.wait()


def attend_call(masks, own, oth, depends, split):
    half, slots, tile, width = own.shape
    keys = 2 * half * tile
    rows = half * tile // (2 if split else 1)
    lanes = min(LANES, rows // 2)
    f32, bf16 = jnp.float32, jnp.bfloat16
    any_ = pl.BlockSpec(memory_space=pl.ANY)
    hbm = pl.BlockSpec(memory_space=pltpu.HBM)
    return pl.pallas_call(
        functools.partial(attend_kernel, STEPS_SPLIT if split else STEPS_WHOLE, lanes, split, len(depends)),
        out_shape=(
            jax.ShapeDtypeStruct((half, slots, tile, width), bf16),
            jax.ShapeDtypeStruct((half, 2, tile, width), bf16),
            jax.ShapeDtypeStruct((half, 2, tile, width), bf16),
        ),
        in_specs=[any_] * (3 + len(depends)),
        out_specs=[hbm, hbm, hbm],
        scratch_shapes=[
            pltpu.VMEM((half, slots - 2, tile, width), bf16),
            pltpu.VMEM((half, slots - 2, tile, width), bf16),
            pltpu.VMEM((2 * half, tile, width), bf16),
            pltpu.VMEM((2 * half, tile, width), bf16),
            pltpu.VMEM((width, keys), bf16),
            pltpu.VMEM((width + 16, keys), bf16),
            pltpu.VMEM((keys, width), f32),
            pltpu.VMEM((keys, width), f32),
            pltpu.VMEM((keys, lanes), f32),
            pltpu.VMEM((keys, lanes), bf16),
            pltpu.VMEM((rows // lanes, 2 * half, lanes), f32),
            pltpu.VMEM((2 * half, 2 * half), jnp.int32),
            pltpu.VMEM((8, lanes), f32),
            pltpu.VMEM((8, lanes), f32),
            pltpu.VMEM((half, 2, tile, width), bf16),
            pltpu.VMEM((half, 2, tile, width), bf16),
            pltpu.SemaphoreType.DMA((6,)),
        ],
        compiler_params=pltpu.CompilerParams(vmem_limit_bytes=(251 if split else 248) * 2**18),
        cost_estimate=pl.CostEstimate(
            flops=12 * rows * keys * width, bytes_accessed=8 * keys * width * 2, transcendentals=rows * keys
        ),
    )(masks, own, oth, *depends)


def join_kernel(rows_ref, keep_ref, taken_ref, *refs):
    send_ref, keep_scr, taken_scr, sum_scr, sems = refs[-5:]
    chips, slots = send_ref.shape[:2]
    parts = sems.shape[1]
    cuts = [pl.ds(n * (chips // parts), chips // parts) for n in range(parts)]
    loads = [
        pltpu.make_async_copy(ref.at[cut], scr.at[cut], sems.at[k, n])
        for n, cut in enumerate(cuts)
        for k, (ref, scr) in enumerate(((keep_ref, keep_scr), (taken_ref, taken_scr)))
    ]
    stores = [
        pltpu.make_async_copy(sum_scr.at[cut], send_ref.at[cut, slots - 2 : slots], sems.at[2, n])
        for n, cut in enumerate(cuts)
    ]
    for load in loads:
        load.start()
    for n in range(parts):
        loads[2 * n].wait()
        loads[2 * n + 1].wait()

        def add(c, _):
            for s in range(2):
                total = keep_scr[c, s].astype(jnp.float32) + taken_scr[c, s].astype(jnp.float32)
                sum_scr[c, s] = total.astype(jnp.bfloat16)
            return 0

        lax.fori_loop(n * (chips // parts), (n + 1) * (chips // parts), add, 0)
        stores[n].start()
    for store in stores:
        store.wait()


def join_call(rows, keep, taken, depends, grant):
    hbm = pl.BlockSpec(memory_space=pltpu.HBM)
    return pl.pallas_call(
        join_kernel,
        out_shape=jax.ShapeDtypeStruct(rows.shape, rows.dtype),
        in_specs=[hbm] + [pl.BlockSpec(memory_space=pl.ANY)] * (2 + len(depends)),
        out_specs=hbm,
        scratch_shapes=[pltpu.VMEM(keep.shape, keep.dtype)] * 3 + [pltpu.SemaphoreType.DMA((3, 4))],
        input_output_aliases={0: 0},
        compiler_params=pltpu.CompilerParams(vmem_limit_bytes=grant),
    )(rows, keep, taken, *depends)


def pack_kernel(chips, width, q_ref, k_ref, v_ref, g_ref, a_ref, b_ref, held, a_scr, b_scr, in_sems, out_sems):
    rows, total = held.shape[1:]
    hr = rows // 2
    copies = [
        pltpu.make_async_copy(ref, held.at[n], in_sems.at[n]) for n, ref in enumerate((q_ref, g_ref, k_ref, v_ref))
    ]
    for copy in copies:
        copy.start()
    sends = []
    for n, copy in enumerate(copies):
        copy.wait()
        for i in range(chips):
            a_scr[i, n] = held[n, :, i * width : (i + 1) * width]
            at = slice((chips + i // 2) * width, (chips + i // 2 + 1) * width)
            if n < 2:
                b_scr[i, 0, n * hr : (n + 1) * hr] = held[n, i % 2 * hr : (i % 2 + 1) * hr, at]
            else:
                b_scr[i, n - 1] = held[n, :, at]
        sends.append(pltpu.make_async_copy(a_scr.at[:, n], a_ref.at[:, n], out_sems.at[n]))
        if n > 0:
            sends.append(pltpu.make_async_copy(b_scr.at[:, n - 1], b_ref.at[:, n - 1], out_sems.at[3 + n]))
        for send in sends[-2 if n else -1 :]:
            send.start()
    for send in sends:
        send.wait()


def pack_call(arrays, chips, width):
    rows, total = arrays[0].shape
    bf16 = jnp.bfloat16
    hbm = pl.BlockSpec(memory_space=pltpu.HBM)
    shapes = [(chips, slots, rows, width) for slots in (4, 3)]
    return pl.pallas_call(
        functools.partial(pack_kernel, chips, width),
        out_shape=[jax.ShapeDtypeStruct(shape, bf16) for shape in shapes],
        in_specs=[hbm] * 4,
        out_specs=[hbm] * 2,
        scratch_shapes=[pltpu.VMEM((4, rows, total), bf16)]
        + [pltpu.VMEM(shape, bf16) for shape in shapes]
        + [pltpu.SemaphoreType.DMA((4,)), pltpu.SemaphoreType.DMA((7,))],
        compiler_params=pltpu.CompilerParams(vmem_limit_bytes=248 * 2**18),
    )(*arrays)


def unpack_whole(width, a_ref, out_ref, query_ref, key_ref, value_ref, got, held, in_sems, out_sems):
    chips = got.shape[1]
    loads = [pltpu.make_async_copy(a_ref.at[:, s], got.at[s], in_sems.at[s]) for s in range(4)]
    for load in loads:
        load.start()
    stores = []
    for s, ref in enumerate((out_ref, query_ref, key_ref, value_ref)):
        loads[s].wait()
        for i in range(chips):
            held[s, :, i * width : (i + 1) * width] = got[s, i]
        stores.append(pltpu.make_async_copy(held.at[s], ref.at[:, 0 : chips * width], out_sems.at[s]))
        stores[s].start()
    for store in stores:
        store.wait()


def unpack_split(width, b_ref, *refs):
    outs, (held, sems) = refs[4:8], refs[8:]
    chips, _, rows, _ = b_ref.shape
    hr = rows // 2
    stores = []
    for s, ref in enumerate(outs):
        for i in range(chips // 2):
            at = slice(i * width, (i + 1) * width)
            if s < 2:
                for part in range(2):
                    held[s, part * hr : (part + 1) * hr, at] = b_ref[2 * i + part, 0, s * hr : (s + 1) * hr]
            else:
                one = b_ref[2 * i, s - 1].astype(jnp.float32) + b_ref[2 * i + 1, s - 1].astype(jnp.float32)
                held[s, :, at] = one.astype(jnp.bfloat16)
        to = ref.at[:, chips * width : chips * width + held.shape[2]]
        stores.append(pltpu.make_async_copy(held.at[s], to, sems.at[s]))
        stores[s].start()
    for store in stores:
        store.wait()


def unpack_call(back_a, back_b, heads):
    chips, _, rows, width = back_a.shape
    bf16 = jnp.bfloat16
    hbm = pl.BlockSpec(memory_space=pltpu.HBM)
    any_ = pl.BlockSpec(memory_space=pl.ANY)
    shapes = [jax.ShapeDtypeStruct((rows, heads * width), bf16)] * 4
    sems = [pltpu.SemaphoreType.DMA((4,)), pltpu.SemaphoreType.DMA((4,))]
    params = pltpu.CompilerParams(vmem_limit_bytes=16 * 2**20)
    whole = pl.pallas_call(
        functools.partial(unpack_whole, width),
        out_shape=shapes,
        in_specs=[any_],
        out_specs=[hbm] * 4,
        scratch_shapes=[pltpu.VMEM((4, chips, rows, width), bf16), pltpu.VMEM((4, rows, chips * width), bf16)] + sems,
        compiler_params=params,
    )(back_a)
    return pl.pallas_call(
        functools.partial(unpack_split, width),
        out_shape=shapes,
        in_specs=[pl.BlockSpec(memory_space=pltpu.VMEM)] + [hbm] * 4,
        out_specs=[hbm] * 4,
        scratch_shapes=[pltpu.VMEM((4, rows, (heads - chips) * width), bf16), pltpu.SemaphoreType.DMA((4,))],
        input_output_aliases={1: 0, 2: 1, 3: 2, 4: 3},
        compiler_params=params,
    )(back_b, *whole)


def after(array, *first):
    hbm = pl.BlockSpec(memory_space=pl.ANY)
    return pl.pallas_call(
        lambda *refs: None,
        out_shape=jax.ShapeDtypeStruct(array.shape, array.dtype),
        in_specs=[hbm] * (1 + len(first)),
        out_specs=hbm,
        input_output_aliases={0: 0},
        compiler_params=pltpu.CompilerParams(vmem_limit_bytes=248 * 2**18),
    )(array, *first)


def body(query, key_in, value, grad_out, masks):
    peers = lax.axis_size("seq")
    chips = peers // 2
    heads = masks.shape[0]
    width = query.shape[1] // heads
    groups = [list(range(e, peers, 2)) for e in range(2)]
    swap = [(i, i ^ 1) for i in range(peers)]

    def exchange(array):
        return lax.all_to_all(array, "seq", 0, 0, axis_index_groups=groups, tiled=True)

    def gather(parts, first, grant):
        rows, keep, give = parts
        return join_call(rows, keep, lax.ppermute(give, "seq", swap), (first,), grant)

    arrays = (query, key_in, value, grad_out)
    send_a, send_b = pack_call(arrays, chips, width)
    got_a = exchange(send_a)
    got_b = exchange(send_b)
    other_a = lax.ppermute(got_a, "seq", swap)
    send_a = gather(attend_call(masks, got_a, other_a, (), False), got_b, 62 * 2**20)
    got_b = after(got_b, send_a)
    other_b = lax.ppermute(got_b, "seq", swap)
    parts_b = attend_call(masks, got_b, other_b, (), True)
    back_a = exchange(send_a)
    rows, keep, give = parts_b
    send_b = join_call(rows, keep, lax.ppermute(give, "seq", swap), (), 62 * 2**20)
    back_b = exchange(after(send_b, back_a))
    return tuple(unpack_call(back_a, back_b, heads))


def solution(mesh):
    tokens = P(("dp", "seq"), None)
    return jax.shard_map(
        body,
        mesh=mesh,
        in_specs=(tokens, tokens, tokens, tokens, P("dp", None, None)),
        out_specs=(tokens, tokens, tokens, tokens),
        check_vma=False,
    )
```

```python
import functools

import jax
import jax.numpy as jnp
from jax import lax
from jax.experimental import pallas as pl
from jax.experimental.pallas import tpu as pltpu
from jax.sharding import PartitionSpec as P

LANES = 512
BLOCK_WHOLE = 256
BLOCK_SPLIT = 512
GROUP = 4096
STEPS_WHOLE = (4096, 4096, 4096, 4096, 4096)
STEPS_SPLIT = (512, 512, 512, 512, 512)
NT = (((1,), (1,)), ((), ()))
NN = (((1,), (0,)), ((), ()))
LOG2E = 1.4426950408889634


def at_multiple(x, n):
    return x if isinstance(x, int) else pl.multiple_of(x, n)


def attend_kernel(
    steps, lanes, split, depends, masks_ref, own_ref, oth_ref, *refs
):
    send_ref, keep_ref, give_ref = refs[depends : depends + 3]
    (rows_scr, qg_scr, k_scr, v_scr, kt_scr, vt_scr, dk_scr, dv_scr, x_scr, p_scr, bias_scr, mask_scr) = refs[depends + 3 : depends + 15]
    (top_scr, stat_scr, give_scr, keep_scr, sems) = refs[depends + 15 :]
    half, slots, tile, width = own_ref.shape
    blocks = 2 * half
    keys = blocks * tile
    queries = half * tile // (2 if split else 1)
    tiles = queries // lanes
    scale = width ** -0.5
    c2 = scale * LOG2E
    ks = slots - 2
    f32, bf16 = jnp.float32, jnp.bfloat16
    per = lanes // tile * (2 if split else 1)
    hr = lanes // per
    tall = vt_scr.shape[0]

    def dot(a, b, dims=NN):
        return lax.dot_general(a, b, dims, preferred_element_type=f32)

    core = lax.axis_index("seq") % 2
    chip = lax.axis_index("seq") // 2
    head = half + chip // 2 if split else chip
    copies = [
        pltpu.make_async_copy(masks_ref.at[head], mask_scr, sems.at[0]),
        pltpu.make_async_copy(own_ref.at[:, ks], k_scr.at[0:half], sems.at[1]),
        pltpu.make_async_copy(oth_ref.at[:, ks], k_scr.at[half:blocks], sems.at[2]),
        pltpu.make_async_copy(own_ref.at[:, 0:ks], qg_scr, sems.at[3]),
        pltpu.make_async_copy(own_ref.at[:, ks + 1], v_scr.at[0:half], sems.at[4]),
        pltpu.make_async_copy(oth_ref.at[:, ks + 1], v_scr.at[half:blocks], sems.at[5]),
    ]
    for copy in copies:
        copy.start()
    copies[0].wait()

    key = lax.broadcasted_iota(jnp.int32, (blocks, blocks), 0)
    from_block = lax.broadcasted_iota(jnp.int32, (blocks, blocks), 1)
    source = 2 * (key % half) + jnp.where(key < half, core, 1 - core)
    pick = (source == from_block).astype(f32).astype(bf16)
    seen = dot(pick, (mask_scr[...] > 0).astype(f32).astype(bf16), NT).astype(bf16)
    lane = lax.broadcasted_iota(jnp.int32, (blocks, lanes), 1)
    row = lax.broadcasted_iota(jnp.int32, (blocks, lanes), 0)
    for t in range(tiles):
        spread = (2 * (lane // hr + per * t) + core == row).astype(f32).astype(bf16)
        bias_scr[t] = jnp.where(dot(seen, spread) > 0.5, 0.0, -1e30)
    for copy in copies[1:]:
        copy.wait()

    def q_tile(t):
        if split:
            return jnp.concatenate([qg_scr[per * t + i, 0, :hr] for i in range(per)], 0)
        return jnp.concatenate([qg_scr[per * t + i, 0] for i in range(per)], 0)

    def g_tile(t):
        if split:
            return jnp.concatenate([qg_scr[per * t + i, 0, hr:] for i in range(per)], 0)
        return jnp.concatenate([qg_scr[per * t + i, 1] for i in range(per)], 0)

    def put(t, slot, x):
        for i in range(per):
            part = x[i * hr : (i + 1) * hr].astype(bf16)
            if split:
                rows_scr[per * t + i, 0, slot * hr : (slot + 1) * hr] = part
            else:
                rows_scr[per * t + i, slot] = part

    def stage(t, scores, probs, grads, step_rows):
        prepare = not probs and not grads
        block = BLOCK_SPLIT if split else BLOCK_WHOLE
        subs = step_rows // block
        if scores:
            q_next = q_tile(t + 1)
        if grads:
            g, q = g_tile(t - 1), q_tile(t - 1)
            delta, inverse = stat_scr[0:1, :], stat_scr[1:2, :].astype(bf16)
        if probs:
            top = jnp.max(top_scr[...], axis=0, keepdims=True) * c2

        def step(i, carry):
            best, o, dq = carry
            group = min(GROUP, step_rows)
            ds_all = []
            for u in range(subs):
                first = i * step_rows + u * block
                sub = pl.ds(at_multiple(first, block), block)
                pair = pl.ds(i * (step_rows // tile) + u * (block // tile), block // tile)
                if grads:
                    pb = p_scr[sub, :] * inverse
                    dp = dot(v_scr[pair].reshape(block, width), g, NT)
                    ds = pb * (dp - delta).astype(bf16)
                    dv_scr[sub, :] += dot(pb, g)
                    dk_scr[sub, :] += dot(ds, q)
                    ds_all.append(ds)
                if probs:
                    pb = jnp.exp2(x_scr[sub, :] * c2 - top).astype(bf16)
                    p_scr[sub, :] = pb
                if scores:
                    s = dot(k_scr[pair].reshape(block, width), q_next, NT).reshape(block // tile, tile, lanes)
                    for w in range(block // tile):
                        x = s[w] + bias_scr[t + 1, pl.ds(i * (step_rows // tile) + u * (block // tile) + w, 1), :]
                        x_scr[pl.ds(at_multiple(first + w * tile, tile), tile), :] = x
                        best = jnp.maximum(best, jnp.max(x.reshape(tile // 8, 8, lanes), axis=0))
                if prepare:
                    for w in range(block // tile):
                        j = i * (step_rows // tile) + u * (block // tile) + w
                        to = pl.ds(at_multiple(first + w * tile, tile), tile)
                        kt_scr[:, to] = k_scr[j].T
                        vt_scr[0:width, to] = v_scr[j].T
                        vt_scr[width:, to] = jnp.ones((tall - width, tile), bf16)
                        dk_scr[to, :] = jnp.zeros((tile, width), f32)
                        dv_scr[to, :] = jnp.zeros((tile, width), f32)
                if (u + 1) * block % group == 0:
                    at = pl.ds(at_multiple(first + block - group, group), group)
                    if grads:
                        dq = dq + dot(kt_scr[:, at], jnp.concatenate(ds_all, 0))
                        ds_all = []
                    if probs:
                        o = o + dot(vt_scr[:, at], p_scr[at, :])
            return best, o, dq

        start = (
            jnp.full((8, lanes), -1e30, f32) if scores else 0,
            jnp.zeros((tall, lanes), f32) if probs else 0,
            jnp.zeros((width, lanes), f32) if grads else 0,
        )
        if keys == step_rows:
            best, o, dq = step(0, start)
        else:
            best, o, dq = lax.fori_loop(0, keys // step_rows, step, start)
        if scores:
            top_scr[...] = best
        if grads:
            put(t - 1, 1, (dq * scale).T)
        if probs:
            rl = 1.0 / o[width : width + 1]
            ot = o[:width] * rl
            put(t, 0, ot.T)
            gf = g_tile(t).astype(f32)
            stat_scr[0:1, :] = jnp.sum(gf.T * ot, axis=0, keepdims=True)
            stat_scr[1:2, :] = rl

    stage(-1, True, False, False, steps[0])
    stage(0, True, True, False, steps[1])

    if tiles > 2:

        def middle(t, _):
            stage(t, True, True, True, steps[2])
            return 0

        lax.fori_loop(1, tiles - 1, middle, 0)
    stage(tiles - 1, False, True, True, steps[3])
    stage(tiles, False, False, True, steps[4])
    rows_out = pltpu.make_async_copy(rows_scr, send_ref.at[:, 0:ks], sems.at[0])
    rows_out.start()

    def finish(base, ref):
        def copy(c, _):
            at = pl.ds(pl.multiple_of((base + c) * tile, tile), tile)
            ref[c, 0] = (dk_scr[at, :] * scale).astype(bf16)
            ref[c, 1] = dv_scr[at, :].astype(bf16)
            return 0

        lax.fori_loop(0, half, copy, 0)

    finish(half, give_scr)
    give_out = pltpu.make_async_copy(give_scr, give_ref, sems.at[1])
    give_out.start()
    finish(0, keep_scr)
    keep_out = pltpu.make_async_copy(keep_scr, keep_ref, sems.at[2])
    keep_out.start()
    rows_out.wait()
    give_out.wait()
    keep_out.wait()


def attend_call(masks, own, oth, depends, split):
    half, slots, tile, width = own.shape
    keys = 2 * half * tile
    rows = half * tile // (2 if split else 1)
    lanes = min(LANES, rows // 2)
    f32, bf16 = jnp.float32, jnp.bfloat16
    any_ = pl.BlockSpec(memory_space=pl.ANY)
    hbm = pl.BlockSpec(memory_space=pltpu.HBM)
    return pl.pallas_call(
        functools.partial(attend_kernel, STEPS_SPLIT if split else STEPS_WHOLE, lanes, split, len(depends)),
        out_shape=(
            jax.ShapeDtypeStruct((half, slots, tile, width), bf16),
            jax.ShapeDtypeStruct((half, 2, tile, width), bf16),
            jax.ShapeDtypeStruct((half, 2, tile, width), bf16),
        ),
        in_specs=[any_] * (3 + len(depends)),
        out_specs=[hbm, hbm, hbm],
        scratch_shapes=[
            pltpu.VMEM((half, slots - 2, tile, width), bf16),
            pltpu.VMEM((half, slots - 2, tile, width), bf16),
            pltpu.VMEM((2 * half, tile, width), bf16),
            pltpu.VMEM((2 * half, tile, width), bf16),
            pltpu.VMEM((width, keys), bf16),
            pltpu.VMEM((width + 16, keys), bf16),
            pltpu.VMEM((keys, width), f32),
            pltpu.VMEM((keys, width), f32),
            pltpu.VMEM((keys, lanes), f32),
            pltpu.VMEM((keys, lanes), bf16),
            pltpu.VMEM((rows // lanes, 2 * half, lanes), f32),
            pltpu.VMEM((2 * half, 2 * half), jnp.int32),
            pltpu.VMEM((8, lanes), f32),
            pltpu.VMEM((8, lanes), f32),
            pltpu.VMEM((half, 2, tile, width), bf16),
            pltpu.VMEM((half, 2, tile, width), bf16),
            pltpu.SemaphoreType.DMA((6,)),
        ],
        compiler_params=pltpu.CompilerParams(vmem_limit_bytes=(251 if split else 248) * 2**18),
        cost_estimate=pl.CostEstimate(
            flops=12 * rows * keys * width, bytes_accessed=8 * keys * width * 2, transcendentals=rows * keys
        ),
    )(masks, own, oth, *depends)


def join_kernel(rows_ref, keep_ref, taken_ref, *refs):
    send_ref, keep_scr, taken_scr, sum_scr, sems = refs[-5:]
    chips, slots = send_ref.shape[:2]
    parts = sems.shape[1]
    cuts = [pl.ds(n * (chips // parts), chips // parts) for n in range(parts)]
    loads = [
        pltpu.make_async_copy(ref.at[cut], scr.at[cut], sems.at[k, n])
        for n, cut in enumerate(cuts)
        for k, (ref, scr) in enumerate(((keep_ref, keep_scr), (taken_ref, taken_scr)))
    ]
    stores = [
        pltpu.make_async_copy(sum_scr.at[cut], send_ref.at[cut, slots - 2 : slots], sems.at[2, n])
        for n, cut in enumerate(cuts)
    ]
    for load in loads:
        load.start()
    for n in range(parts):
        loads[2 * n].wait()
        loads[2 * n + 1].wait()

        def add(c, _):
            for s in range(2):
                total = keep_scr[c, s].astype(jnp.float32) + taken_scr[c, s].astype(jnp.float32)
                sum_scr[c, s] = total.astype(jnp.bfloat16)
            return 0

        lax.fori_loop(n * (chips // parts), (n + 1) * (chips // parts), add, 0)
        stores[n].start()
    for store in stores:
        store.wait()


def join_call(rows, keep, taken, depends, grant):
    hbm = pl.BlockSpec(memory_space=pltpu.HBM)
    return pl.pallas_call(
        join_kernel,
        out_shape=jax.ShapeDtypeStruct(rows.shape, rows.dtype),
        in_specs=[hbm] + [pl.BlockSpec(memory_space=pl.ANY)] * (2 + len(depends)),
        out_specs=hbm,
        scratch_shapes=[pltpu.VMEM(keep.shape, keep.dtype)] * 3 + [pltpu.SemaphoreType.DMA((3, 4))],
        input_output_aliases={0: 0},
        compiler_params=pltpu.CompilerParams(vmem_limit_bytes=grant),
    )(rows, keep, taken, *depends)


def pack_kernel(chips, width, q_ref, k_ref, v_ref, g_ref, a_ref, b_ref, held, a_scr, b_scr, in_sems, out_sems):
    rows, total = held.shape[1:]
    hr = rows // 2
    copies = [
        pltpu.make_async_copy(ref, held.at[n], in_sems.at[n]) for n, ref in enumerate((q_ref, g_ref, k_ref, v_ref))
    ]
    for copy in copies:
        copy.start()
    sends = []
    for n, copy in enumerate(copies):
        copy.wait()
        for i in range(chips):
            a_scr[i, n] = held[n, :, i * width : (i + 1) * width]
            at = slice((chips + i // 2) * width, (chips + i // 2 + 1) * width)
            if n < 2:
                b_scr[i, 0, n * hr : (n + 1) * hr] = held[n, i % 2 * hr : (i % 2 + 1) * hr, at]
            else:
                b_scr[i, n - 1] = held[n, :, at]
        sends.append(pltpu.make_async_copy(a_scr.at[:, n], a_ref.at[:, n], out_sems.at[n]))
        if n > 0:
            sends.append(pltpu.make_async_copy(b_scr.at[:, n - 1], b_ref.at[:, n - 1], out_sems.at[3 + n]))
        for send in sends[-2 if n else -1 :]:
            send.start()
    for send in sends:
        send.wait()


def pack_call(arrays, chips, width):
    rows, total = arrays[0].shape
    bf16 = jnp.bfloat16
    hbm = pl.BlockSpec(memory_space=pltpu.HBM)
    shapes = [(chips, slots, rows, width) for slots in (4, 3)]
    return pl.pallas_call(
        functools.partial(pack_kernel, chips, width),
        out_shape=[jax.ShapeDtypeStruct(shape, bf16) for shape in shapes],
        in_specs=[hbm] * 4,
        out_specs=[hbm] * 2,
        scratch_shapes=[pltpu.VMEM((4, rows, total), bf16)]
        + [pltpu.VMEM(shape, bf16) for shape in shapes]
        + [pltpu.SemaphoreType.DMA((4,)), pltpu.SemaphoreType.DMA((7,))],
        compiler_params=pltpu.CompilerParams(vmem_limit_bytes=248 * 2**18),
    )(*arrays)


def unpack_whole(width, a_ref, out_ref, query_ref, key_ref, value_ref, got, held, in_sems, out_sems):
    chips = got.shape[1]
    loads = [pltpu.make_async_copy(a_ref.at[:, s], got.at[s], in_sems.at[s]) for s in range(4)]
    for load in loads:
        load.start()
    stores = []
    for s, ref in enumerate((out_ref, query_ref, key_ref, value_ref)):
        loads[s].wait()
        for i in range(chips):
            held[s, :, i * width : (i + 1) * width] = got[s, i]
        stores.append(pltpu.make_async_copy(held.at[s], ref.at[:, 0 : chips * width], out_sems.at[s]))
        stores[s].start()
    for store in stores:
        store.wait()


def unpack_split(width, b_ref, *refs):
    outs, (held, sems) = refs[4:8], refs[8:]
    chips, _, rows, _ = b_ref.shape
    hr = rows // 2
    stores = []
    for s, ref in enumerate(outs):
        for i in range(chips // 2):
            at = slice(i * width, (i + 1) * width)
            if s < 2:
                for part in range(2):
                    held[s, part * hr : (part + 1) * hr, at] = b_ref[2 * i + part, 0, s * hr : (s + 1) * hr]
            else:
                one = b_ref[2 * i, s - 1].astype(jnp.float32) + b_ref[2 * i + 1, s - 1].astype(jnp.float32)
                held[s, :, at] = one.astype(jnp.bfloat16)
        to = ref.at[:, chips * width : chips * width + held.shape[2]]
        stores.append(pltpu.make_async_copy(held.at[s], to, sems.at[s]))
        stores[s].start()
    for store in stores:
        store.wait()


def unpack_call(back_a, back_b, heads):
    chips, _, rows, width = back_a.shape
    bf16 = jnp.bfloat16
    hbm = pl.BlockSpec(memory_space=pltpu.HBM)
    any_ = pl.BlockSpec(memory_space=pl.ANY)
    shapes = [jax.ShapeDtypeStruct((rows, heads * width), bf16)] * 4
    sems = [pltpu.SemaphoreType.DMA((4,)), pltpu.SemaphoreType.DMA((4,))]
    params = pltpu.CompilerParams(vmem_limit_bytes=16 * 2**20)
    whole = pl.pallas_call(
        functools.partial(unpack_whole, width),
        out_shape=shapes,
        in_specs=[any_],
        out_specs=[hbm] * 4,
        scratch_shapes=[pltpu.VMEM((4, chips, rows, width), bf16), pltpu.VMEM((4, rows, chips * width), bf16)] + sems,
        compiler_params=params,
    )(back_a)
    return pl.pallas_call(
        functools.partial(unpack_split, width),
        out_shape=shapes,
        in_specs=[pl.BlockSpec(memory_space=pltpu.VMEM)] + [hbm] * 4,
        out_specs=[hbm] * 4,
        scratch_shapes=[pltpu.VMEM((4, rows, (heads - chips) * width), bf16), pltpu.SemaphoreType.DMA((4,))],
        input_output_aliases={1: 0, 2: 1, 3: 2, 4: 3},
        compiler_params=params,
    )(back_b, *whole)


def after(array, *first):
    hbm = pl.BlockSpec(memory_space=pl.ANY)
    return pl.pallas_call(
        lambda *refs: None,
        out_shape=jax.ShapeDtypeStruct(array.shape, array.dtype),
        in_specs=[hbm] * (1 + len(first)),
        out_specs=hbm,
        input_output_aliases={0: 0},
        compiler_params=pltpu.CompilerParams(vmem_limit_bytes=248 * 2**18),
    )(array, *first)


def body(query, key_in, value, grad_out, masks):
    peers = lax.axis_size("seq")
    chips = peers // 2
    heads = masks.shape[0]
    width = query.shape[1] // heads
    groups = [list(range(e, peers, 2)) for e in range(2)]
    swap = [(i, i ^ 1) for i in range(peers)]

    def exchange(array):
        return lax.all_to_all(array, "seq", 0, 0, axis_index_groups=groups, tiled=True)

    def gather(parts, first, grant):
        rows, keep, give = parts
        return join_call(rows, keep, lax.ppermute(give, "seq", swap), (first,), grant)

    arrays = (query, key_in, value, grad_out)
    send_a, send_b = pack_call(arrays, chips, width)
    got_a = exchange(send_a)
    got_b = exchange(send_b)
    other_a = lax.ppermute(got_a, "seq", swap)
    send_a = gather(attend_call(masks, got_a, other_a, (), False), got_b, 62 * 2**20)
    got_b = after(got_b, send_a)
    other_b = lax.ppermute(got_b, "seq", swap)
    parts_b = attend_call(masks, got_b, other_b, (), True)
    back_a = exchange(send_a)
    rows, keep, give = parts_b
    send_b = join_call(rows, keep, lax.ppermute(give, "seq", swap), (), 62 * 2**20)
    back_b = exchange(after(send_b, back_a))
    return tuple(unpack_call(back_a, back_b, heads))


def solution(mesh):
    tokens = P(("dp", "seq"), None)
    return jax.shard_map(
        body,
        mesh=mesh,
        in_specs=(tokens, tokens, tokens, tokens, P("dp", None, None)),
        out_specs=(tokens, tokens, tokens, tokens),
        check_vma=False,
    )
```
